32 devices in a mesh: seq: 4 (over y, core), blk: 8 (over z, x).
Axes of the slice: x: 2, y: 2, z: 4, core: 2. Of those that a mesh axis runs over, the one named last changes fastest.
Arguments:
- inputs: bfloat16 [2, 3072, 2048], P(None, ('seq', 'blk')), may hold values from -6 to 6
- seg_ids: int32 [2, 3072], P(None, 'seq'), may hold values from 0 to 1, as said below
- norm_in: bfloat16 [2048], P(('seq', 'blk')), may hold values from 0.099609375 to 1.8984375
- proj_y: bfloat16 [2048, 2560], P(('seq', 'blk')), may hold values from -0.125 to 0.125
- proj_x: bfloat16 [2048, 2560], P(('seq', 'blk')), may hold values from -0.125 to 0.125
- conv_weight: float32 [4, 2560], P(None, 'blk'), may hold values from -3 to 3
- conv_bias: float32 [2560], P('blk'), may hold values from -2 to 2
- rate_weight: bfloat16 [16, 160, 160], P('blk'), may hold values from -0.5 to 0.5
- rate_bias: float32 [2560], P('blk'), may hold values from -4 to 4
- input_weight: bfloat16 [16, 160, 160], P('blk'), may hold values from -0.5 to 0.5
- input_bias: float32 [2560], P('blk'), may hold values from -4 to 4
- decay_param: float32 [2560], P('blk'), may hold values from 3 to 12
- proj_out: bfloat16 [2048, 2560], P(('seq', 'blk')), may hold values from -0.5 to 0.5
- norm_mlp: bfloat16 [2048], P(('seq', 'blk')), may hold values from 0.099609375 to 1.8984375
- mlp_gate: bfloat16 [2048, 6144], P(('seq', 'blk')), may hold values from -0.125 to 0.125
- mlp_up: bfloat16 [2048, 6144], P(('seq', 'blk')), may hold values from -0.125 to 0.125
- mlp_down: bfloat16 [2048, 6144], P(('seq', 'blk')), may hold values from -0.15625 to 0.15625
- cotangent: bfloat16 [2, 3072, 2048], P(None, ('seq', 'blk')), may hold values from -6 to 6
Outputs:
- output: bfloat16 [2, 3072, 2048], P(None, ('seq', 'blk'))
- grad_inputs: bfloat16 [2, 3072, 2048], P(None, ('seq', 'blk'))
- grad_norm_in: float32 [2048], P(('seq', 'blk'))
- grad_proj_y: float32 [2048, 2560], P(('seq', 'blk'))
- grad_proj_x: float32 [2048, 2560], P(('seq', 'blk'))
- grad_conv_weight: float32 [4, 2560], P(None, 'blk')
- grad_conv_bias: float32 [2560], P('blk')
- grad_rate_weight: float32 [16, 160, 160], P('blk')
- grad_rate_bias: float32 [2560], P('blk')
- grad_input_weight: float32 [16, 160, 160], P('blk')
- grad_input_bias: float32 [2560], P('blk')
- grad_decay_param: float32 [2560], P('blk')
- grad_proj_out: float32 [2048, 2560], P(('seq', 'blk'))
- grad_norm_mlp: float32 [2048], P(('seq', 'blk'))
- grad_mlp_gate: float32 [2048, 6144], P(('seq', 'blk'))
- grad_mlp_up: float32 [2048, 6144], P(('seq', 'blk'))
- grad_mlp_down: float32 [2048, 6144], P(('seq', 'blk'))
The draws below stay inside these ranges and needn't reach their ends.
Inputs may be any that keep to these rules, and one draw needn't show every extreme that they name: `seg_ids`: for each micro-batch and sequence group, ids are 0 before a cut and 1 from it on, the cut lying after the group's first token; each group holds two sequences.
All inputs are finite; a program needn't handle non-finite values.
Results may differ from the reference program's by a relative error of at most 0.014.
Values may be sent and summed in bfloat16 or wider, within the bound.
No kernel may reach another device: no remote copies, remote signals or barrier semaphores. Data moves between devices by JAX's collectives and lax.ppermute only.
A program may use at most 576 MiB of HBM per device.

```python
from functools import partial
import jax
import jax.numpy as jnp
from jax import lax

D = 2048
HEADS = 16
BW = 160
FF = 6144
CONV = 4
MICRO = 2
RNN = 2560
GROUP_TOK = 768
TOKENS = 3072
N_SEQ = 4


def draw_seg_ids(key, part):
    key = jax.random.fold_in(key, 11)
    cut_points = jax.random.randint(key, (MICRO, N_SEQ, 1), 1, GROUP_TOK)
    positions = jnp.arange(GROUP_TOK, dtype=jnp.int32)[None, None, :]
    return (positions >= cut_points).astype(jnp.int32).reshape(MICRO, N_SEQ * GROUP_TOK)


def draw_decay_param(key, part):
    key = jax.random.fold_in(key, 23)
    return jax.random.uniform(key, (RNN,), jnp.float32, 3.0, 11.0)


def level_of(rng, extent, cuts, least, high):
    gain, own = 1.0, jax.random.fold_in(rng, 6)
    for dim, parts in cuts:
        draws = jnp.exp(jax.random.uniform(jax.random.fold_in(own, dim), (parts,), jnp.float32, least / len(cuts), high / len(cuts)))
        gain = gain * jnp.repeat(draws, extent[dim] // parts).reshape([-1 if axis == dim else 1 for axis in range(len(extent))])
    return gain


def bell_draw(own_key, dims, deviation, bound, shards=(), held_as=jnp.bfloat16):
    result = deviation * jax.random.normal(own_key, dims, jnp.float32)
    if shards:
        result = result * level_of(own_key, dims, shards, -0.22, 0.18)
    return jnp.clip(result, -bound, bound).astype(held_as)


def setup_inputs(seed: int = 0) -> dict:
    key_of = jax.random.split(jax.random.key(seed), 19)
    inputs = bell_draw(key_of[0], (MICRO, TOKENS, D), 1.0, 6.0, ((1, 32),))
    seg_ids = draw_seg_ids(jax.random.fold_in(key_of[18], 71), 0)
    norm_in = jnp.clip(1.0 + 0.18 * jax.random.normal(key_of[2], (D,), jnp.float32), 0.099609375, 1.8984375).astype(jnp.bfloat16)
    proj_y = bell_draw(key_of[3], (D, RNN), D ** -0.5, 0.125, ((0, 32),))
    proj_x = bell_draw(key_of[4], (D, RNN), D ** -0.5, 0.125, ((0, 32),))
    conv_weight = bell_draw(key_of[5], (CONV, RNN), 0.5, 3.0, ((1, 8),), jnp.float32)
    conv_bias = bell_draw(key_of[6], (RNN,), 0.3, 2.0, ((0, 8),), jnp.float32)
    rate_weight = bell_draw(key_of[7], (HEADS, BW, BW), BW ** -0.5, 0.5, ((0, 8),))
    rate_bias = bell_draw(key_of[8], (RNN,), 1.0, 4.0, ((0, 8),), jnp.float32)
    input_weight = bell_draw(key_of[9], (HEADS, BW, BW), BW ** -0.5, 0.5, ((0, 8),))
    input_bias = bell_draw(key_of[10], (RNN,), 1.0, 4.0, ((0, 8),), jnp.float32)
    decay_param = draw_decay_param(jax.random.fold_in(key_of[18], 71), 0)
    proj_out = bell_draw(key_of[12], (D, RNN), (RNN // 16) ** -0.5, 0.5, ((0, 32),))
    norm_mlp = jnp.clip(1.0 + 0.18 * jax.random.normal(key_of[13], (D,), jnp.float32), 0.099609375, 1.8984375).astype(jnp.bfloat16)
    mlp_gate = bell_draw(key_of[14], (D, FF), D ** -0.5, 0.125, ((0, 32),))
    mlp_up = bell_draw(key_of[15], (D, FF), D ** -0.5, 0.125, ((0, 32),))
    mlp_down = bell_draw(key_of[16], (D, FF), (FF // 4) ** -0.5, 0.15625, ((0, 32),))
    cotangent = bell_draw(key_of[17], (MICRO, TOKENS, D), 1.0, 6.0, ((1, 32),))
    return dict(inputs=inputs, seg_ids=seg_ids, norm_in=norm_in, proj_y=proj_y, proj_x=proj_x, conv_weight=conv_weight, conv_bias=conv_bias, rate_weight=rate_weight, rate_bias=rate_bias, input_weight=input_weight, input_bias=input_bias, decay_param=decay_param, proj_out=proj_out, norm_mlp=norm_mlp, mlp_gate=mlp_gate, mlp_up=mlp_up, mlp_down=mlp_down, cotangent=cotangent)


NORM_EPS = 1e-06

@jax.custom_vjp
def low(v):
    return lax.optimization_barrier(v.astype(jnp.bfloat16)).astype(jnp.float32)

@jax.custom_vjp
def low_back(v):
    return v

def low_keep(v):
    return (low(v), None)

def low_pass(kept, grad):
    return (grad,)

def back_keep(v):
    return (v, None)

def back_low(kept, grad):
    return (low(grad),)
low.defvjp(low_keep, low_pass)
low_back.defvjp(back_keep, back_low)

def recurrence(values, segments, conv_weight, conv_bias, rate_weight, rate_bias, input_weight, input_bias, decay_param):
    taps = conv_weight.shape[0]
    length = values.shape[1]
    filtered = conv_bias + values * conv_weight[0]
    for offset in range(1, taps):
        shifted = jnp.pad(values, ((0, 0), (offset, 0), (0, 0)))[:, :length]
        same_doc = jnp.pad(segments, ((0, 0), (offset, 0)), constant_values=-1)[:, :length] == segments
        filtered = filtered + jnp.where(same_doc[..., None], shifted, 0.0) * conv_weight[offset]
    blocks = rate_weight.shape[0]
    block_width = rate_weight.shape[1]
    grouped = filtered.reshape(filtered.shape[0], length, blocks, block_width)
    pre_rate = jnp.einsum('blhi,hij->blhj', grouped, rate_weight, precision=lax.Precision.HIGHEST).reshape(filtered.shape) + rate_bias
    pre_input = jnp.einsum('blhi,hij->blhj', grouped, input_weight, precision=lax.Precision.HIGHEST).reshape(filtered.shape) + input_bias
    rate_gate = jax.nn.sigmoid(pre_rate)
    input_gate = jax.nn.sigmoid(pre_input)
    log_decay = -8.0 * rate_gate * jax.nn.softplus(-decay_param)
    previous = jnp.pad(segments, ((0, 0), (1, 0)), constant_values=-1)[:, :length]
    seg_start = previous != segments
    decay_now = jnp.where(seg_start[..., None], 0.0, jnp.exp(log_decay))
    input_scale = jnp.sqrt(-jnp.expm1(2.0 * log_decay))
    driven = input_scale * input_gate * filtered

    def combine(earlier, later):
        return (earlier[0] * later[0], later[0] * earlier[1] + later[1])
    scanned = lax.associative_scan(combine, (decay_now, driven), axis=1)
    return scanned[1]

def rms_norm(rows_in, gain_vec):
    return rows_in * lax.rsqrt(lax.optimization_barrier(jnp.mean(rows_in * rows_in, axis=-1, keepdims=True)) + NORM_EPS) * gain_vec

def matmul(left, right):
    return jnp.einsum('mtd,df->mtf', left, right, precision=lax.Precision.HIGHEST)

def matmul_back(left, right):
    return jnp.einsum('mtf,df->mtd', left, right, precision=lax.Precision.HIGHEST)

def forward(seg_ids, inputs, norm_in, proj_y, proj_x, conv_weight, conv_bias, rate_weight, rate_bias, input_weight, input_bias, decay_param, proj_out, norm_mlp, mlp_gate, mlp_up, mlp_down):
    normed = low(rms_norm(inputs, norm_in))
    branch_y = jax.nn.gelu(low_back(matmul(normed, proj_y)))
    drive_in = low_back(low(matmul(normed, proj_x)))
    grouped = drive_in.reshape(MICRO * N_SEQ, GROUP_TOK, RNN)
    segments = seg_ids.reshape(MICRO * N_SEQ, GROUP_TOK)
    scan_state = recurrence(grouped, segments, conv_weight, conv_bias, rate_weight, rate_bias, input_weight, input_bias, decay_param)
    hidden_val = low_back(low(scan_state.reshape(MICRO, TOKENS, RNN)))
    mixed_in = low(branch_y * hidden_val)
    resid = inputs + low_back(matmul_back(mixed_in, proj_out))
    normed_mlp = low(rms_norm(resid, norm_mlp))
    pre_gate = low_back(matmul(normed_mlp, mlp_gate))
    pre_up = low_back(matmul(normed_mlp, mlp_up))
    product = low(jax.nn.gelu(pre_gate) * pre_up)
    return resid + low_back(matmul_back(product, mlp_down))

def reference(inputs, seg_ids, norm_in, proj_y, proj_x, conv_weight, conv_bias, rate_weight, rate_bias, input_weight, input_bias, decay_param, proj_out, norm_mlp, mlp_gate, mlp_up, mlp_down, cotangent):
    floats = tuple((a.astype(jnp.float32) for a in (inputs, norm_in, proj_y, proj_x, conv_weight, conv_bias, rate_weight, rate_bias, input_weight, input_bias, decay_param, proj_out, norm_mlp, mlp_gate, mlp_up, mlp_down)))
    block_out, pullback = jax.vjp(partial(forward, seg_ids), *floats)
    grads = pullback(cotangent.astype(jnp.float32))
    return (block_out.astype(jnp.bfloat16), grads[0].astype(jnp.bfloat16), grads[1], grads[2], grads[3], grads[4], grads[5], grads[6], grads[7], grads[8], grads[9], grads[10], grads[11], grads[12], grads[13], grads[14], grads[15])
```

```python
import functools

import jax
import jax.numpy as jnp
from jax import lax
from jax.experimental import pallas as pl
from jax.experimental.pallas import tpu as pltpu
from jax.sharding import PartitionSpec as P

NORM_EPS = 1e-06
F32 = jnp.float32
BF16 = jnp.bfloat16
TAPS = 4
HALO = 8


class Grid:
    def __init__(self, n_seq, n_blk):
        core = 2 if n_seq % 2 == 0 else 1
        nx = max(d for d in range(1, n_blk + 1) if d * d <= n_blk and n_blk % d == 0)
        self.n = {"y": n_seq // core, "c": core, "z": n_blk // nx, "x": nx}
        self.n_blk = n_blk

    def index(self, part):
        seq, blk = lax.axis_index("seq"), lax.axis_index("blk")
        return {
            "y": seq // self.n["c"],
            "c": seq % self.n["c"],
            "z": blk // self.n["x"],
            "x": blk % self.n["x"],
        }[part]

    def shift(self, value, part, by, wrap=True):
        outer, inner, axis = {
            "y": ("y", "c", "seq"),
            "c": ("y", "c", "seq"),
            "z": ("z", "x", "blk"),
            "x": ("z", "x", "blk"),
        }[part]
        pairs = []
        for o in range(self.n[outer]):
            for i in range(self.n[inner]):
                p = (o if part == outer else i) + by
                if not wrap and not 0 <= p < self.n[part]:
                    continue
                p = p % self.n[part]
                to = (p, i) if part == outer else (o, p)
                pairs.append((o * self.n[inner] + i, to[0] * self.n[inner] + to[1]))
        return lax.ppermute(value, axis, pairs)

    def gather_abs(self, value, part, ring=False):
        n, me = self.n[part], self.index(part)
        out = jnp.zeros((n, *value.shape), value.dtype)
        held = value
        for r in range(n):
            if r:
                held = self.shift(held, part, 1) if ring else self.shift(value, part, r)
            out = lax.dynamic_update_index_in_dim(out, held, (me - r) % n, 0)
        return out

    def scatter_sum(self, value, part, dim):
        n, me = self.n[part], self.index(part)
        total = lax.dynamic_index_in_dim(value, me, dim, keepdims=False)
        for r in range(1, n):
            piece = lax.dynamic_index_in_dim(value, (me + r) % n, dim, keepdims=False)
            total = total + self.shift(piece, part, r)
        return total

    def total(self, value, part):
        out = value.astype(F32)
        for r in range(1, self.n[part]):
            out = out + self.shift(value, part, r).astype(F32)
        return out.astype(value.dtype)

    def spread(self, shard, first):
        nx, ny = self.n["x"], self.n["y"]
        got = {(0, 0): shard}
        for r in range(1, nx):
            got[0, r] = self.shift(shard, "x", r)
        for r in range(1, ny):
            got[r, 0] = self.shift(shard, "y", r)
        for ry in range(1, ny):
            for rx in range(1, nx):
                if first == "x":
                    got[ry, rx] = self.shift(got[0, rx], "y", ry)
                else:
                    got[ry, rx] = self.shift(got[ry, 0], "x", rx)
        return jnp.concatenate([got[ry, rx] for ry in range(ny) for rx in range(nx)], axis=0)

    def collect(self, partial, first):
        nx, ny = self.n["x"], self.n["y"]
        part = partial.reshape(ny, nx, partial.shape[0] // (ny * nx), partial.shape[1])
        total = part[0, 0].astype(F32)
        if first == "y":
            for rx in range(1, nx):
                held = part[0, rx]
                if ny > 1:
                    held = held.astype(F32)
                    for ry in range(1, ny):
                        held = held + self.shift(part[ry, rx], "y", -ry).astype(F32)
                total = total + self.shift(held.astype(BF16), "x", -rx).astype(F32)
            for ry in range(1, ny):
                total = total + self.shift(part[ry, 0], "y", -ry).astype(F32)
        else:
            for ry in range(1, ny):
                held = part[ry, 0]
                if nx > 1:
                    held = held.astype(F32)
                    for rx in range(1, nx):
                        held = held + self.shift(part[ry, rx], "x", -rx).astype(F32)
                total = total + self.shift(held.astype(BF16), "y", -ry).astype(F32)
            for rx in range(1, nx):
                total = total + self.shift(part[0, rx], "x", -rx).astype(F32)
        return total

    def columns_of(self, pieces):
        nx, ny, nz, nc = self.n["x"], self.n["y"], self.n["z"], self.n["c"]
        x, y, z, c = (self.index(p) for p in "xyzc")
        rows = pieces[0].shape[0]

        def take(yy, xx):
            out = []
            for w in pieces:
                width = w.shape[1] // (nx * ny)
                out.append(lax.dynamic_slice_in_dim(w, (yy * nx + xx) * width, width, 1))
            return out[0] if len(out) == 1 else jnp.concatenate(out, axis=1)

        def for_x(xx):
            return jnp.stack([take(yy, xx) for yy in range(ny)])

        width = sum(w.shape[1] for w in pieces) // (nx * ny)
        mine = jnp.zeros((ny, nx, rows, width), BF16)
        for r in range(nx):
            got = for_x((x + r) % nx)
            if r:
                got = self.shift(got, "x", r)
            mine = lax.dynamic_update_slice_in_dim(mine, got[:, None], (x - r) % nx, 1)
        block = jnp.zeros((ny, nx, rows, width), BF16)
        for r in range(ny):
            got = lax.dynamic_index_in_dim(mine, (y + r) % ny, 0, keepdims=False)
            if r:
                got = self.shift(got, "y", r)
            block = lax.dynamic_update_index_in_dim(block, got, (y - r) % ny, 0)
        whole = jnp.zeros((ny, nc, nz, nx * rows, width), BF16)
        held = block.reshape(ny, 1, 1, nx * rows, width)
        for r in range(nz):
            if r:
                held = self.shift(held, "z", 1)
            for s in range(nc):
                other = self.shift(held, "c", s) if s else held
                whole = lax.dynamic_update_slice(whole, other, (0, (c - s) % nc, (z - r) % nz, 0, 0))
        return whole.reshape(ny * nc * nz * nx * rows, width)

    def weight_grad(self, left, right, widths):
        nx, ny, nz, nc = self.n["x"], self.n["y"], self.n["z"], self.n["c"]
        x, y, z, c = (self.index(p) for p in "xyzc")
        tokens, depth = left.shape
        rows = depth // (nx * ny * nz * nc)
        wide = left.reshape(tokens, ny, nc, nz, nx * rows)

        def part(core):
            cut = lax.dynamic_index_in_dim(wide, core, 2, keepdims=False)
            cut = cut.transpose(0, 2, 1, 3).reshape(tokens, depth // nc)
            return cut

        def product(core):
            return lax.dot_general(
                part(core), right, (((0,), (0,)), ((), ())), preferred_element_type=F32
            )

        mine = product(c)
        for s in range(1, nc):
            mine = mine + self.shift(product((c + s) % nc).astype(BF16), "c", s).astype(F32)
        mine = mine.reshape(nz, depth // (nc * nz), right.shape[1])

        def slab(r):
            return lax.dynamic_index_in_dim(mine, (z - r) % nz, 0, keepdims=False)

        if nz > 1:
            held = slab(1).astype(BF16)
            for r in range(2, nz):
                held = (slab(r) + self.shift(held, "z", 1).astype(F32)).astype(BF16)
            done = slab(0) + self.shift(held, "z", 1).astype(F32)
        else:
            done = slab(0)
        done = done.astype(BF16).reshape(ny, nx, rows, right.shape[1])
        side = jnp.zeros((ny, nx, rows, right.shape[1]), BF16)
        for r in range(ny):
            got = lax.dynamic_index_in_dim(done, (y + r) % ny, 0, keepdims=False)
            if r:
                got = self.shift(got, "y", r)
            side = lax.dynamic_update_index_in_dim(side, got, (y - r) % ny, 0)
        outs = [jnp.zeros((rows, w * nx * ny), F32) for w in widths]
        for r in range(nx):
            got = lax.dynamic_index_in_dim(side, (x + r) % nx, 1, keepdims=False)
            if r:
                got = self.shift(got, "x", r)
            got = got.astype(F32)
            for yy in range(ny):
                at = 0
                for i, w in enumerate(widths):
                    column = (yy * nx + (x - r) % nx) * w
                    outs[i] = lax.dynamic_update_slice(
                        outs[i], got[yy, :, at : at + w], (0, column)
                    )
                    at += w
        return outs


def decay_terms(rate, slope):
    log_decay = rate * slope
    small = 1.0 / 40320.0
    for div in (5040.0, 720.0, 120.0, 24.0, 6.0, 2.0, 1.0):
        small = small * log_decay + 1.0 / div
    less = jnp.where(log_decay < -0.4, jnp.exp(log_decay) - 1.0, log_decay * small)
    decay = 1.0 + less
    square = -less * (1.0 + decay)
    return decay, square


def split_dot(value, weight):
    high = value.astype(BF16)
    rest = (value - high.astype(F32)).astype(BF16)
    return jnp.dot(high, weight, preferred_element_type=F32) + jnp.dot(
        rest, weight, preferred_element_type=F32
    )


def forward_kernel(order, u, halo, same, vec, gates, conv, rate, gate_in, state, prods, ends, rows, keep_a, keep_b):
    nx, step = u.shape[1], u.shape[2]
    length = nx * step
    rows[0:HALO] = halo[0]
    for i in range(nx):
        rows[HALO + i * step : HALO + (i + 1) * step] = u[0, order[i]].astype(F32)
    filtered = vec[4:5] + rows[HALO : HALO + length] * vec[0:1]
    for k in range(1, TAPS):
        filtered = filtered + rows[HALO - k : HALO - k + length] * same[0, :, k : k + 1] * vec[k : k + 1]
    conv[0] = filtered
    r_gate = jax.nn.sigmoid(split_dot(filtered, gates[0]) + vec[5:6])
    i_gate = jax.nn.sigmoid(split_dot(filtered, gates[1]) + vec[6:7])
    rate[0] = r_gate
    gate_in[0] = i_gate
    decay, square = decay_terms(r_gate, vec[7:8])
    a = decay * same[0, :, 1:2]
    b = jnp.sqrt(square) * i_gate * filtered
    width = a.shape[1]
    tiles = length // 8
    a = a.reshape(tiles, 8, width)
    b = b.reshape(tiles, 8, width)
    row = lax.broadcasted_iota(jnp.int32, (tiles, 8, width), 1)
    for d in (1, 2, 4):
        a_back = jnp.where(row >= d, pltpu.roll(a, d, 1), 1.0)
        b_back = jnp.where(row >= d, pltpu.roll(b, d, 1), 0.0)
        b = b + a * b_back
        a = a * a_back
    keep_a[...] = a.reshape(length, width)
    keep_b[...] = b.reshape(length, width)
    carry_s = jnp.zeros((1, width), F32)
    carry_a = jnp.ones((1, width), F32)
    for t in range(tiles):
        at = keep_a[t * 8 : t * 8 + 8]
        bt = keep_b[t * 8 : t * 8 + 8]
        s = bt + at * carry_s
        p = at * carry_a
        state[0, t * 8 : t * 8 + 8] = s
        prods[0, t * 8 : t * 8 + 8] = p
        carry_s = s[7:8]
        carry_a = p[7:8]
    ends[0, 0:1] = carry_a
    ends[0, 1:2] = carry_s
    ends[0, 2:8] = jnp.zeros((6, width), F32)


def reverse_kernel(order, d_state, same, vec, rate, grads, prods, ends, keep_g, keep_a):
    nx, step = d_state.shape[1], d_state.shape[2]
    length = nx * step
    width = rate.shape[2]
    decay, _ = decay_terms(rate[0], vec[7:8])
    a = decay * same[0, :, 1:2]
    keep_a[0:length] = a
    keep_a[length : length + 8] = jnp.ones((8, width), F32)
    for i in range(nx):
        keep_g[i * step : (i + 1) * step] = d_state[0, order[i]].astype(F32)
    first = a[0:1]
    tiles = length // 8
    nxt = keep_a[1 : length + 1].reshape(tiles, 8, width)
    g = keep_g[...].reshape(tiles, 8, width)
    row = lax.broadcasted_iota(jnp.int32, (tiles, 8, width), 1)
    p = nxt
    for d in (1, 2, 4):
        g_ahead = jnp.where(row < 8 - d, pltpu.roll(g, 8 - d, 1), 0.0)
        p_ahead = jnp.where(row < 8 - d, pltpu.roll(p, 8 - d, 1), 1.0)
        g = g + p * g_ahead
        p = p * p_ahead
    keep_g[...] = g.reshape(length, width)
    keep_a[0:length] = p.reshape(length, width)
    carry_g = jnp.zeros((1, width), F32)
    carry_p = jnp.ones((1, width), F32)
    for t in reversed(range(tiles)):
        pt = keep_a[t * 8 : t * 8 + 8]
        gt = keep_g[t * 8 : t * 8 + 8] + pt * carry_g
        pt = pt * carry_p
        grads[0, t * 8 : t * 8 + 8] = gt
        prods[0, t * 8 : t * 8 + 8] = pt
        carry_g = gt[0:1]
        carry_p = pt[0:1]
    ends[0, 0:1] = first * carry_p
    ends[0, 1:2] = first * carry_g
    ends[0, 2:8] = jnp.zeros((6, width), F32)


def final_kernel(
    order, u, halo, same, vec, gates, conv, rate, gate_in, state, prods, start, grads, back, carry,
    d_u, head, d_rate, d_input, sums, rows, tail,
):
    nx, step = u.shape[1], u.shape[2]
    length = nx * step
    width = conv.shape[2]
    d_s = grads[0] + back[0] * carry[0, 0:1]
    s_now = state[0] + prods[0] * start[0, 0:1]
    rows[HALO : HALO + length] = s_now
    rows[HALO - 1 : HALO] = start[0, 0:1]
    s_prev = rows[HALO - 1 : HALO - 1 + length]
    r_gate, i_gate, filtered = rate[0], gate_in[0], conv[0]
    decay, square = decay_terms(r_gate, vec[7:8])
    inverse = lax.rsqrt(jnp.maximum(square, 1e-37))
    scale = square * inverse
    a = decay * same[0, :, 1:2]
    d_scaled = d_s * i_gate * filtered
    d_log = d_s * s_prev * a - d_scaled * (decay * decay) * inverse
    d_i = d_s * scale * filtered * i_gate * (1.0 - i_gate)
    d_r = d_log * vec[7:8] * r_gate * (1.0 - r_gate)
    d_r_low = d_r.astype(BF16)
    d_i_low = d_i.astype(BF16)
    d_rate[0] = d_r_low
    d_input[0] = d_i_low
    back_dims = (((1,), (1,)), ((), ()))
    d_c = (
        d_s * scale * i_gate
        + lax.dot_general(d_r_low, gates[0], back_dims, preferred_element_type=F32)
        + lax.dot_general(d_i_low, gates[1], back_dims, preferred_element_type=F32)
    )
    rows[0:HALO] = halo[0]
    for i in range(nx):
        rows[HALO + i * step : HALO + (i + 1) * step] = u[0, order[i]].astype(F32)

    def column(value):
        return jnp.sum(value, axis=0, keepdims=True)

    parts = [column(d_c * rows[HALO : HALO + length])]
    tail[0:HALO] = jnp.zeros((HALO, width), F32)
    tail[HALO + length : 2 * HALO + length] = jnp.zeros((HALO, width), F32)
    d_rows = d_c * vec[0:1]
    d_head = jnp.zeros((HALO, width), F32)
    for k in range(1, TAPS):
        masked = d_c * same[0, :, k : k + 1]
        parts.append(column(masked * rows[HALO - k : HALO - k + length]))
        tail[HALO : HALO + length] = masked * vec[k : k + 1]
        d_rows = d_rows + tail[HALO + k : HALO + k + length]
        d_head = d_head + tail[k : k + HALO]
    for i in range(nx):
        d_u[0, order[i]] = d_rows[i * step : (i + 1) * step]
    head[0] = d_head
    parts += [column(d_c), column(d_r), column(d_i), column(d_log * r_gate)]

    @pl.when(pl.program_id(0) == 0)
    def _():
        sums[...] = jnp.zeros_like(sums)

    for i, value in enumerate(parts):
        sums[i : i + 1] += value


def chain_spec(*dims):
    return pl.BlockSpec((1, *dims), lambda i: (i,) + (0,) * len(dims))


def whole_spec(*dims):
    return pl.BlockSpec(dims, lambda i: (0,) * len(dims))


def scan_call(kernel, chains, operands, outs, scratch, flops):
    specs = [pl.BlockSpec(memory_space=pltpu.SMEM)]
    for value, chained in operands[1:]:
        specs.append(chain_spec(*value.shape[1:]) if chained else whole_spec(*value.shape))
    shapes, out_specs = [], []
    for shape, dtype, chained in outs:
        shapes.append(jax.ShapeDtypeStruct(shape, dtype))
        out_specs.append(chain_spec(*shape[1:]) if chained else whole_spec(*shape))
    moved = sum(v.size * v.dtype.itemsize for v, _ in operands)
    moved += sum(s.size * s.dtype.itemsize for s in shapes)
    return pl.pallas_call(
        kernel,
        grid=(chains,),
        in_specs=specs,
        out_specs=out_specs,
        out_shape=shapes,
        scratch_shapes=[pltpu.VMEM(s, F32) for s in scratch],
        compiler_params=pltpu.CompilerParams(vmem_limit_bytes=48 * 1024 * 1024),
        cost_estimate=pl.CostEstimate(flops=flops, bytes_accessed=moved, transcendentals=0),
    )(*[v for v, _ in operands])


def norm_back(grad_in, rows_in, scale_vec, gain_vec):
    weighted = grad_in * gain_vec
    return scale_vec * weighted - rows_in * scale_vec**3 * jnp.mean(
        weighted * rows_in, axis=-1, keepdims=True
    )


def mix(left, right):
    return jnp.dot(left, right, preferred_element_type=F32)


def mix_back(left, right):
    return lax.dot_general(left, right, (((1,), (1,)), ((), ())), preferred_element_type=F32)


def on_device(
    grid,
    inputs,
    seg_ids,
    norm_in,
    proj_y,
    proj_x,
    conv_weight,
    conv_bias,
    rate_weight,
    rate_bias,
    input_weight,
    input_bias,
    decay_param,
    proj_out,
    norm_mlp,
    mlp_gate,
    mlp_up,
    mlp_down,
    cotangent,
):
    nx, ny, nz, nc = (grid.n[p] for p in "xyzc")
    x, y, z, c = (grid.index(p) for p in "xyzc")
    planes = nx * ny
    micro, step, depth = inputs.shape
    chains = micro * ny
    length = nx * step
    local = planes * step
    firsts = ["x" if m % 2 == 0 else "y" for m in range(micro)]

    def spread(shard):
        return jnp.concatenate(
            [grid.spread(shard[m], firsts[m]) for m in range(micro)], axis=0
        )

    def collect(partial):
        partial = partial.reshape(micro, local, partial.shape[1])
        return jnp.stack(
            [grid.collect(partial[m], "y" if firsts[m] == "x" else "x") for m in range(micro)]
        )

    source = inputs.astype(F32)
    rows_in = spread(inputs)
    mix_x = grid.columns_of([proj_x])
    mix_y = grid.columns_of([proj_y])
    mix_out = grid.columns_of([proj_out])
    width = mix_x.shape[1]
    ff_in = grid.columns_of([mlp_gate, mlp_up])
    ff_down = grid.columns_of([mlp_down])
    ff_width = ff_down.shape[1]
    rows_cot = spread(cotangent)

    slope = -8.0 * jax.nn.softplus(-decay_param)
    slope_back = 8.0 * jax.nn.sigmoid(-decay_param)
    small = jnp.concatenate(
        [
            conv_weight,
            conv_bias[None],
            rate_bias[None],
            input_bias[None],
            slope[None],
        ],
        axis=0,
    )
    share = small.shape[1]
    gain_pair = jnp.stack([norm_in, norm_mlp]).astype(F32)
    gate_pair = jnp.stack([rate_weight, input_weight], axis=1)
    heads, block = gate_pair.shape[0], gate_pair.shape[2]
    per = nz // ny

    def own_channels(value):
        by_z = grid.gather_abs(value, "z", ring=True)
        part = lax.dynamic_slice_in_dim(by_z, y * per, per, 0)
        by_x = grid.gather_abs(part, "x")
        flat = jnp.moveaxis(by_x, 0, 1).reshape(per * nx, *value.shape)
        return lax.dynamic_slice_in_dim(flat, x * per, per, 0)

    vec = jnp.moveaxis(own_channels(small), 0, 1).reshape(8, width)
    gate_own = own_channels(gate_pair).reshape(per * heads, 2, block, block)
    dense = [jnp.zeros((width, width), BF16) for _ in range(2)]
    for h in range(per * heads):
        for g in range(2):
            dense[g] = lax.dynamic_update_slice(dense[g], gate_own[h, g], (h * block, h * block))
    gates = jnp.stack(dense)
    gains = gain_pair
    for part in "xzcy":
        gains = grid.gather_abs(gains, part)
    gains = jnp.moveaxis(gains, -2, 0).reshape(2, depth)
    gain_in, gain_mlp = gains[0], gains[1]

    segments = jnp.stack([seg_ids] + [grid.shift(seg_ids, "y", r) for r in range(1, ny)], axis=1)
    padded = jnp.pad(segments, ((0, 0), (0, 0), (HALO, 0)), constant_values=-1)
    near = lax.dynamic_slice_in_dim(padded, z * length, length + HALO, 2)
    here = near[:, :, HALO:]
    same = [jnp.ones_like(here, dtype=F32)]
    for k in range(1, TAPS):
        same.append((near[:, :, HALO - k : HALO - k + length] == here).astype(F32))
    same = jnp.stack(same + [jnp.zeros_like(same[0])] * (8 - TAPS), axis=-1)
    same = same.reshape(chains, length, 8)
    order = ((x - jnp.arange(nx, dtype=jnp.int32)) % nx).astype(jnp.int32)

    wide = rows_in.astype(F32)
    scale_wide = lax.rsqrt(jnp.mean(wide * wide, axis=-1, keepdims=True) + NORM_EPS)
    normed = (wide * scale_wide * gain_in).astype(BF16)
    drive = mix(normed, mix_x).astype(BF16).reshape(chains, nx, step, width)
    pre_y = mix(normed, mix_y)
    branch_y, gelu_y_back = jax.vjp(jax.nn.gelu, pre_y)
    last = lax.dynamic_index_in_dim(drive, (x - (nx - 1)) % nx, 1, keepdims=False)
    halo = grid.shift(last[:, step - HALO :].astype(F32), "z", 1, wrap=False)
    shape = (chains, length, width)
    conv, rate, gate_in, state, prods, ends = scan_call(
        forward_kernel,
        chains,
        [(order, False), (drive, True), (halo, True), (same, True), (vec, False), (gates, False)],
        [(shape, F32, True)] * 5 + [((chains, 8, width), F32, True)],
        [(length + HALO, width), (length, width), (length, width)],
        flops=8 * chains * length * width * width,
    )

    def carry_from(summary, sign):
        carry = jnp.zeros((chains, 1, width), F32)
        for r in reversed(range(1, nz)):
            got = grid.shift(summary, "z", sign * r, wrap=False)
            carry = got[:, 1:2] + got[:, 0:1] * carry
        return carry

    start = carry_from(ends[:, 0:2], 1)
    hidden = (state + prods * start).astype(BF16).reshape(chains, nx, step, width)

    def relative(value):
        return jnp.concatenate(
            [
                lax.dynamic_index_in_dim(value, (x - r) % nx, 1, keepdims=True) for r in range(nx)
            ],
            axis=1,
        ).reshape(chains * length, width)

    hidden_f = relative(hidden).astype(F32)
    mixed = (branch_y * hidden_f).astype(BF16)
    resid = source + collect(mix_back(mixed, mix_out).astype(BF16))

    scale_mlp = lax.rsqrt(jnp.mean(resid * resid, axis=-1, keepdims=True) + NORM_EPS)
    normed_mlp = spread((resid * scale_mlp * gain_mlp).astype(BF16))
    pre_ff = mix(normed_mlp, ff_in)
    pre_gate, pre_up = pre_ff[:, :ff_width], pre_ff[:, ff_width:]
    activated, gelu_gate_back = jax.vjp(jax.nn.gelu, pre_gate)
    product = (activated * pre_up).astype(BF16)
    grad_prod = mix(rows_cot, ff_down)
    grad_gate = gelu_gate_back(grad_prod * pre_up)[0].astype(BF16)
    grad_up = (grad_prod * activated).astype(BF16)
    grad_ff = jnp.concatenate([grad_gate, grad_up], axis=1)
    grad_norm_mlp = collect(mix_back(grad_ff, ff_in).astype(BF16))
    block_out = (resid + collect(mix_back(product, ff_down).astype(BF16))).astype(BF16)
    grad_gate_w, grad_up_w = grid.weight_grad(normed_mlp, grad_ff, [ff_width, ff_width])
    (grad_down_w,) = grid.weight_grad(rows_cot, product, [ff_width])
    term_gain_mlp = jnp.sum(grad_norm_mlp * resid * scale_mlp, axis=(0, 1))
    grad_resid = cotangent.astype(F32) + norm_back(grad_norm_mlp, resid, scale_mlp, gain_mlp)
    grad_branch = spread(grad_resid.astype(BF16))

    grad_mixed = mix(grad_branch, mix_out)
    grad_pre_y = gelu_y_back(grad_mixed * hidden_f)[0].astype(BF16)
    grad_state = (grad_mixed * branch_y).astype(BF16).reshape(chains, nx, step, width)
    d_local, d_prods, d_ends = scan_call(
        reverse_kernel,
        chains,
        [(order, False), (grad_state, True), (same, True), (vec, False), (rate, True)],
        [(shape, F32, True)] * 2 + [((chains, 8, width), F32, True)],
        [(length, width), (length + HALO, width)],
        flops=40 * chains * length * width,
    )
    d_carry = carry_from(d_ends[:, 0:2], -1)
    d_drive, head, *d_pre, sums = scan_call(
        final_kernel,
        chains,
        [
            (order, False),
            (drive, True),
            (halo, True),
            (same, True),
            (vec, False),
            (gates, False),
            (conv, True),
            (rate, True),
            (gate_in, True),
            (state, True),
            (prods, True),
            (start, True),
            (d_local, True),
            (d_prods, True),
            (d_carry, True),
        ],
        [
            ((chains, nx, step, width), F32, True),
            ((chains, HALO, width), F32, True),
            (shape, BF16, True),
            (shape, BF16, True),
            ((8, width), F32, False),
        ],
        [(length + HALO, width), (length + 2 * HALO, width)],
        flops=8 * chains * length * width * width,
    )
    after = grid.shift(head, "z", -1, wrap=False)
    chunk = lax.broadcasted_iota(jnp.int32, (1, nx, 1, 1), 1)
    tail = jnp.pad(after, ((0, 0), (step - HALO, 0), (0, 0)))[:, None]
    d_drive = d_drive + jnp.where(chunk == (x - (nx - 1)) % nx, tail, 0.0)
    grad_drive = d_drive.astype(BF16).reshape(chains * length, width)
    both = jnp.concatenate([grad_pre_y, grad_drive], axis=1)
    grad_normed = collect(
        (mix_back(grad_pre_y, mix_y) + mix_back(grad_drive, mix_x)).astype(BF16)
    )
    grad_y_w, grad_x_w = grid.weight_grad(normed, both, [width, width])
    (grad_out_w,) = grid.weight_grad(grad_branch, mixed, [width])
    scale_in = lax.rsqrt(jnp.mean(source * source, axis=-1, keepdims=True) + NORM_EPS)
    term_gain_in = jnp.sum(grad_normed * source * scale_in, axis=(0, 1))
    grad_source = (grad_resid + norm_back(grad_normed, source, scale_in, gain_in)).astype(BF16)

    terms = jnp.stack([term_gain_in, term_gain_mlp]).reshape(2, ny, nc, nz, nx, -1)
    for part, dim in (("c", 2), ("y", 1), ("z", 1), ("x", 1)):
        terms = grid.scatter_sum(terms, part, dim)
    conv_low = conv.reshape(chains * length, width).astype(BF16)
    gate_dense = [
        lax.dot_general(
            conv_low,
            d.reshape(chains * length, width),
            (((0,), (0,)), ((), ())),
            preferred_element_type=F32,
        )
        for d in d_pre
    ]
    gate_grads = jnp.stack(
        [
            jnp.stack([d[h * block : (h + 1) * block, h * block : (h + 1) * block] for d in gate_dense])
            for h in range(per * heads)
        ]
    )

    def own_share(value):
        value = grid.total(grid.total(value, "c"), "z")
        by_y = grid.gather_abs(grid.gather_abs(value, "x"), "y")
        flat = by_y.reshape(ny * nx * per, *value.shape[1:])
        return lax.dynamic_index_in_dim(flat, z * nx + x, 0, keepdims=False)

    gate_share = own_share(gate_grads.astype(BF16).reshape(per, heads, 2, block, block)).astype(F32)
    sum_share = own_share(jnp.moveaxis(sums.reshape(8, per, share), 0, 1))
    return (
        block_out,
        grad_source,
        terms[0],
        grad_y_w,
        grad_x_w,
        sum_share[0:4],
        sum_share[4],
        gate_share[:, 0],
        sum_share[5],
        gate_share[:, 1],
        sum_share[6],
        sum_share[7] * slope_back,
        grad_out_w,
        terms[1],
        grad_gate_w,
        grad_up_w,
        grad_down_w,
    )


def solution(mesh):
    grid = Grid(mesh.shape["seq"], mesh.shape["blk"])
    every = ("seq", "blk")
    placed = (
        P(None, every, None),
        P(None, "seq"),
        P(every),
        P(every, None),
        P(every, None),
        P(None, "blk"),
        P("blk"),
        P("blk", None, None),
        P("blk"),
        P("blk", None, None),
        P("blk"),
        P("blk"),
        P(every, None),
        P(every),
        P(every, None),
        P(every, None),
        P(every, None),
        P(None, every, None),
    )
    return jax.shard_map(
        functools.partial(on_device, grid),
        mesh=mesh,
        in_specs=placed,
        out_specs=(
            P(None, every, None),
            P(None, every, None),
            P(every),
            P(every, None),
            P(every, None),
            P(None, "blk"),
            P("blk"),
            P("blk", None, None),
            P("blk"),
            P("blk", None, None),
            P("blk"),
            P("blk"),
            P(every, None),
            P(every),
            P(every, None),
            P(every, None),
            P(every, None),
        ),
        check_vma=False,
    )
```

```python
import functools

import jax
import jax.numpy as jnp
from jax import lax
from jax.experimental import pallas as pl
from jax.experimental.pallas import tpu as pltpu
from jax.sharding import PartitionSpec as P

NORM_EPS = 1e-06
F32 = jnp.float32
BF16 = jnp.bfloat16
TAPS = 4
HALO = 8


class Grid:
    def __init__(self, n_seq, n_blk):
        core = 2 if n_seq % 2 == 0 else 1
        nx = max(d for d in range(1, n_blk + 1) if d * d <= n_blk and n_blk % d == 0)
        self.n = {"y": n_seq // core, "c": core, "z": n_blk // nx, "x": nx}
        self.n_blk = n_blk

    def index(self, part):
        seq, blk = lax.axis_index("seq"), lax.axis_index("blk")
        return {
            "y": seq // self.n["c"],
            "c": seq % self.n["c"],
            "z": blk // self.n["x"],
            "x": blk % self.n["x"],
        }[part]

    def shift(self, value, part, by, wrap=True):
        outer, inner, axis = {
            "y": ("y", "c", "seq"),
            "c": ("y", "c", "seq"),
            "z": ("z", "x", "blk"),
            "x": ("z", "x", "blk"),
        }[part]
        pairs = []
        for o in range(self.n[outer]):
            for i in range(self.n[inner]):
                p = (o if part == outer else i) + by
                if not wrap and not 0 <= p < self.n[part]:
                    continue
                p = p % self.n[part]
                to = (p, i) if part == outer else (o, p)
                pairs.append((o * self.n[inner] + i, to[0] * self.n[inner] + to[1]))
        return lax.ppermute(value, axis, pairs)

    def shift_plane(self, value, by_y, by_x):
        ny, nc, nz, nx = (self.n[p] for p in "yczx")
        pairs = []
        for y in range(ny):
            for c in range(nc):
                for z in range(nz):
                    for x in range(nx):
                        to = (((y + by_y) % ny * nc + c) * nz + z) * nx + (x + by_x) % nx
                        pairs.append((((y * nc + c) * nz + z) * nx + x, to))
        return lax.ppermute(value, ("seq", "blk"), pairs)

    def place(self, by_shift, part):
        n, me = self.n[part], self.index(part)
        if n == 1:
            return by_shift[0][None]
        if n == 2:
            here, there = by_shift
            low = me == 0
            return jnp.stack([jnp.where(low, here, there), jnp.where(low, there, here)])
        out = jnp.zeros((n, *by_shift[0].shape), by_shift[0].dtype)
        for r, value in enumerate(by_shift):
            out = lax.dynamic_update_index_in_dim(out, value, (me - r) % n, 0)
        return out

    def gather(self, value, part):
        n = self.n[part]
        return self.place([value] + [self.shift(value, part, r) for r in range(1, n)], part)

    def exchange(self, value, part, dim):
        n, me = self.n[part], self.index(part)
        got = []
        for r in range(n):
            piece = lax.dynamic_index_in_dim(value, (me + r) % n, dim, keepdims=False)
            got.append(self.shift(piece, part, r) if r else piece)
        return self.place(got, part)

    def total(self, value, part, *late):
        out = value.astype(F32)
        for r in range(1, self.n[part]):
            out = out + after(self.shift(value, part, r), *late).astype(F32)
        return out.astype(value.dtype)

    def turn(self, value, back=False):
        ny, nc, nz = self.n["y"], self.n["c"], self.n["z"]
        places = [
            (y * nc + c) * nz + z for c in range(nc) for z in range(nz) for y in range(ny)
        ]
        width = value.shape[-1] // len(places)
        if width % 128:
            cut = value.reshape(*value.shape[:-1], *((nc, nz, ny) if back else (ny, nc, nz)), width)
            k = value.ndim - 1
            order = (k + 2, k, k + 1) if back else (k + 1, k + 2, k)
            return cut.transpose(tuple(range(k)) + order + (k + 3,)).reshape(value.shape)

        def kernel(src, dst):
            for k, place in enumerate(places):
                here, there = pl.ds(k * width, width), pl.ds(place * width, width)
                if back:
                    dst[:, :, there] = src[:, :, here]
                else:
                    dst[:, :, here] = src[:, :, there]

        return pl.pallas_call(
            kernel,
            out_shape=jax.ShapeDtypeStruct(value.shape, value.dtype),
            cost_estimate=pl.CostEstimate(flops=0, bytes_accessed=4 * value.size, transcendentals=0),
        )(value)

    def spread(self, shard, *late, normed=False):
        nx, ny = self.n["x"], self.n["y"]
        micro, step, width = shard.shape
        got = {(0, 0): shard}
        for r in range(1, nx):
            got[0, r] = after(self.shift(shard, "x", r), *late)
        for r in range(1, ny):
            got[r, 0] = after(self.shift(shard, "y", r), *late)
        hop = [v for k, v in got.items() if k != (0, 0)]
        out = []
        for m in range(micro):
            for ry in range(ny):
                for rx in range(nx):
                    if ry == 0 or rx == 0:
                        out.append((got[ry, rx], m))
                    elif m % 2 == 0:
                        out.append((self.shift(got[0, rx][m], "y", ry), None))
                    else:
                        out.append((self.shift(got[ry, 0][m], "x", rx), None))
        rows = assemble_rows(out, step, width, normed)
        return rows.reshape(len(out) * step, width), hop

    def collect(self, partial, micro):
        nx, ny = self.n["x"], self.n["y"]
        part = partial.reshape(micro, ny, nx, -1, partial.shape[1])
        out = []
        for m in range(micro):
            if m % 2 == 0:
                held = part[m, 0].astype(F32)
                for r in range(1, ny):
                    held = held + self.shift(part[m, r], "y", -r).astype(F32)
                last, n = "x", nx
            else:
                held = part[m, :, 0].astype(F32)
                for r in range(1, nx):
                    held = held + self.shift(part[m, :, r], "x", -r).astype(F32)
                last, n = "y", ny
            total = held[0]
            for r in range(1, n):
                total = total + self.shift(held[r].astype(BF16), last, -r).astype(F32)
            out.append(total)
        return jnp.stack(out)

    def columns_of(self, pieces, *late):
        nx, ny = self.n["x"], self.n["y"]
        x, y = self.index("x"), self.index("y")

        def take(yy, xx):
            out = []
            for w in pieces:
                width = w.shape[1] // (nx * ny)
                out.append(lax.dynamic_slice_in_dim(w, (yy * nx + xx) * width, width, 1))
            return out[0] if len(out) == 1 else jnp.concatenate(out, axis=1)

        rows = []
        for ry in range(ny):
            got = []
            for rx in range(nx):
                piece = take((y + ry) % ny, (x + rx) % nx)
                got.append(after(self.shift_plane(piece, ry, rx), *late) if ry or rx else piece)
            rows.append(self.place(got, "x"))
        return self.place(rows, "y")

    def ring_first(self, block):
        if self.n["z"] != 4:
            return (self.shift(block, "z", -1),)
        return self.shift(block, "z", -1), self.shift(block, "z", 1)

    def ring_rest(self, block, first, *late):
        nz = self.n["z"]
        first = [after(v, *late) for v in first]
        if nz != 4:
            out = [block, first[0]]
            for _ in range(2, nz):
                out.append(self.shift(out[-1], "z", -1))
            return out[:nz]
        half = block.shape[0] // 2
        above, below = first
        far = [self.shift(above[:half], "z", -1), self.shift(below[half:], "z", 1)]
        return [block, above, *far, below]

    def whole_rows(self, pieces, *cuts):
        nc, nz = self.n["c"], self.n["z"]
        c, z = self.index("c"), self.index("z")
        block = sum(p.shape[0] for p in pieces) // nz
        starts = [sum(p.shape[0] for p in pieces[:i]) for i in range(len(pieces))]
        parts, places = [], []
        for s in range(nc):
            parts += [self.shift(p, "c", -s) if s else p for p in pieces]
            for at in starts:
                where = ((c + s) % nc * nz + (z + at // block) % nz) * block + at % block
                places.append(where)
        places = jnp.stack(places).astype(jnp.int32)
        return [assemble_tall(parts, places, i, len(cuts)) for i in cuts]

    def z_groups(self):
        nz, nx = self.n["z"], self.n["x"]
        return [[z * nx + x for z in range(nz)] for x in range(nx)]

    def all_rows(self, block):
        ny, nc, nz, nx = (self.n[p] for p in "yczx")
        groups = [
            [((y * nc + c) * nz + z) * nx + x for c in range(nc) for z in range(nz)]
            for y in range(ny)
            for x in range(nx)
        ]
        return lax.all_gather(
            block, ("seq", "blk"), axis=0, tiled=True, axis_index_groups=groups
        )

    def to_owners(self, done, *late):
        nx, ny = self.n["x"], self.n["y"]
        x, y = self.index("x"), self.index("y")
        rows = []
        for ry in range(ny):
            got = []
            for rx in range(nx):
                piece = lax.dynamic_slice(
                    done, ((y + ry) % ny, (x + rx) % nx, 0, 0), (1, 1, *done.shape[2:])
                )[0, 0]
                got.append(after(self.shift_plane(piece, ry, rx), *late) if ry or rx else piece)
            rows.append(self.place(got, "x"))
        return self.place(rows, "y")


class WeightSum:
    def __init__(self, grid, left, right):
        self.grid, self.left, self.right = grid, left, right
        self.share = left.shape[1] // grid.n["c"]

    def product(self, core):
        cut = lax.dynamic_slice_in_dim(self.left, core * self.share, self.share, 1)
        return lax.dot_general(
            cut, self.right, (((0,), (0,)), ((), ())), preferred_element_type=F32
        )

    def meet(self):
        grid, nc = self.grid, self.grid.n["c"]
        c = grid.index("c")
        others = [
            grid.shift(self.product((c + s) % nc).astype(BF16), "c", s) for s in range(1, nc)
        ]
        mine = self.product(c)
        for other in others:
            mine = mine + other.astype(F32)
        self.mine = mine

    def along_z(self, *late):
        self.done = lax.psum_scatter(
            after(self.mine.astype(BF16), *late),
            "blk",
            scatter_dimension=0,
            tiled=True,
            axis_index_groups=self.grid.z_groups(),
        )

    def slab(self, r):
        nz = self.grid.n["z"]
        rows = self.share // nz
        at = (self.grid.index("z") + r) % nz * rows
        return lax.dynamic_slice_in_dim(self.mine, at, rows, 0)

    def step_one(self, *late):
        low = after(self.slab(2).astype(BF16), *late)
        half = low.shape[0] // 2
        self.first = [
            self.grid.shift(low[:half], "z", 1),
            self.grid.shift(low[half:], "z", -1),
        ]

    def step_two(self, *late):
        grid = self.grid
        up, down = [after(v, *late).astype(F32) for v in self.first]
        half = up.shape[0]
        above, below = self.slab(1), self.slab(3)
        to_up = jnp.concatenate([above[:half] + up, above[half:]], axis=0).astype(BF16)
        to_down = jnp.concatenate([below[:half], below[half:] + down], axis=0).astype(BF16)
        self.second = [grid.shift(to_up, "z", 1), grid.shift(to_down, "z", -1)]

    def join(self, *late):
        second = [after(v, *late).astype(F32) for v in self.second]
        self.done = (self.slab(0) + (second[0] + second[1])).astype(BF16)

    def finish(self, count, *late):
        grid = self.grid
        ny, nx = grid.n["y"], grid.n["x"]
        width = self.done.shape[1] // count
        done = after(self.done, *late).reshape(ny, nx, -1, self.done.shape[1])
        side = grid.to_owners(done)
        return [
            jnp.concatenate(
                [
                    side[yy, xx, :, i * width : (i + 1) * width].astype(F32)
                    for yy in range(ny)
                    for xx in range(nx)
                ],
                axis=1,
            )
            for i in range(count)
        ]


def after(value, *others):
    return lax.optimization_barrier((value, *others))[0]


def assemble_rows(pieces, step, width, normed):
    arrays = []
    for value, _ in pieces:
        if not any(value is a for a in arrays):
            arrays.append(value)
    which = [next(i for i, a in enumerate(arrays) if a is value) for value, _ in pieces]
    cut = 32 if step % 32 == 0 else step

    def kernel(*refs):
        out = refs[-1]
        for k, (_, lead) in enumerate(pieces):
            ref = refs[which[k]]
            block = ref[...] if lead is None else ref[lead]
            if normed:
                block = block.astype(F32)
                square = jnp.mean(block * block, axis=-1, keepdims=True)
                block = (block * lax.rsqrt(square + NORM_EPS)).astype(out.dtype)
            out[k] = block

    specs = []
    for a in arrays:
        if a.ndim == 2:
            specs.append(pl.BlockSpec((cut, width), lambda i: (i, 0)))
        else:
            specs.append(pl.BlockSpec((a.shape[0], cut, width), lambda i: (0, i, 0)))
    count = len(pieces)
    return pl.pallas_call(
        kernel,
        grid=(step // cut,),
        in_specs=specs,
        out_specs=pl.BlockSpec((count, cut, width), lambda i: (0, i, 0)),
        out_shape=jax.ShapeDtypeStruct((count, step, width), BF16),
        compiler_params=pltpu.CompilerParams(vmem_limit_bytes=32 * 1024 * 1024),
        cost_estimate=pl.CostEstimate(
            flops=0, bytes_accessed=4 * count * step * width, transcendentals=0
        ),
    )(*arrays)


def assemble_tall(pieces, places, part, parts):
    width = pieces[0].shape[1] // parts
    total = sum(p.shape[0] for p in pieces)
    cut = next((t for t in (512, 640, 128) if width % t == 0), width)
    steps = width // cut

    def kernel(where, *refs):
        out = refs[-1]
        for i, ref in enumerate(refs[:-1]):
            out[pl.ds(pl.multiple_of(where[i], 64), ref.shape[0])] = ref[...]

    if cut % 128 and parts > 1:
        pieces = [p[:, part * width : (part + 1) * width] for p in pieces]
        part = 0
    return pl.pallas_call(
        kernel,
        grid_spec=pltpu.PrefetchScalarGridSpec(
            num_scalar_prefetch=1,
            grid=(steps,),
            in_specs=[
                pl.BlockSpec((p.shape[0], cut), lambda i, where: (0, i + part * steps))
                for p in pieces
            ],
            out_specs=pl.BlockSpec((total, cut), lambda i, where: (0, i)),
        ),
        out_shape=jax.ShapeDtypeStruct((total, width), BF16),
        compiler_params=pltpu.CompilerParams(vmem_limit_bytes=32 * 1024 * 1024),
        cost_estimate=pl.CostEstimate(flops=0, bytes_accessed=4 * total * width, transcendentals=0),
    )(places, *pieces)


def pack_small(rate_weight, input_weight, small):
    heads, block, _ = rate_weight.shape
    rows = heads * block
    by_head = jnp.moveaxis(small.reshape(8, heads, block), 1, 0)
    by_head = jnp.pad(by_head, ((0, 0), (0, 8), (0, 0))).reshape(heads * 16, block)

    def kernel(rate, gate_in, values, out):
        for h in range(heads):
            out[0, h * block : (h + 1) * block] = rate[h]
            out[1, h * block : (h + 1) * block] = gate_in[h]
        rest = values[...]
        for t in range(3):
            high = rest.astype(BF16)
            at = rows + t * heads * 16
            out[0, at : at + heads * 16] = high
            out[1, at : at + heads * 16] = high
            rest = rest - high.astype(F32)

    return pl.pallas_call(
        kernel,
        out_shape=jax.ShapeDtypeStruct((2, rows + 48 * heads, block), BF16),
        cost_estimate=pl.CostEstimate(flops=0, bytes_accessed=8 * rows * block, transcendentals=0),
    )(rate_weight, input_weight, by_head)


def unpack_small(halves, place, per, heads):
    _, _, depth, block = halves.shape
    rows = heads * block
    width = per * rows

    def kernel(which, share, gates, vec):
        row = lax.broadcasted_iota(jnp.int32, (block, width), 0)
        column = lax.broadcasted_iota(jnp.int32, (block, width), 1)
        total = jnp.zeros((16, width), F32)
        for p in range(per):
            for h in range(heads):
                head = p * heads + h
                pick = jnp.where(column == row + head * block, 1.0, 0.0).astype(BF16)
                for g in range(2):
                    part = share[g, p, h * block : (h + 1) * block]
                    gates[g, head * block : (head + 1) * block] = jnp.dot(
                        part, pick, preferred_element_type=F32
                    ).astype(BF16)
                for t in range(3):
                    at = rows + (t * heads + h) * 16
                    total = total + jnp.dot(
                        share[0, p, at : at + 16], pick, preferred_element_type=F32
                    )
        vec[...] = total[0:8]

    return pl.pallas_call(
        kernel,
        grid_spec=pltpu.PrefetchScalarGridSpec(
            num_scalar_prefetch=1,
            grid=(1,),
            in_specs=[pl.BlockSpec((2, per, depth, block), lambda i, which: (0, which[0], 0, 0))],
            out_specs=[
                pl.BlockSpec((2, width, width), lambda i, which: (0, 0, 0)),
                pl.BlockSpec((8, width), lambda i, which: (0, 0)),
            ],
        ),
        out_shape=[
            jax.ShapeDtypeStruct((2, width, width), BF16),
            jax.ShapeDtypeStruct((8, width), F32),
        ],
        compiler_params=pltpu.CompilerParams(vmem_limit_bytes=32 * 1024 * 1024),
        cost_estimate=pl.CostEstimate(
            flops=0, bytes_accessed=4 * width * width, transcendentals=0
        ),
    )(place.astype(jnp.int32)[None], halves)


def decay_terms(rate, slope):
    log_decay = rate * slope
    small = 1.0 / 40320.0
    for div in (5040.0, 720.0, 120.0, 24.0, 6.0, 2.0, 1.0):
        small = small * log_decay + 1.0 / div
    less = jnp.where(log_decay < -0.4, jnp.exp(log_decay) - 1.0, log_decay * small)
    decay = 1.0 + less
    square = -less * (1.0 + decay)
    return decay, square


def split_dot(value, weight):
    high = value.astype(BF16)
    rest = (value - high.astype(F32)).astype(BF16)
    return jnp.dot(high, weight, preferred_element_type=F32) + jnp.dot(
        rest, weight, preferred_element_type=F32
    )


def forward_kernel(order, u, halo, same, vec, gates, conv, rate, gate_in, state, prods, ends, rows, keep_a, keep_b):
    nx, step = u.shape[1], u.shape[2]
    length = nx * step
    rows[0:HALO] = halo[0]
    for i in range(nx):
        rows[HALO + i * step : HALO + (i + 1) * step] = u[0, order[i]].astype(F32)
    filtered = vec[4:5] + rows[HALO : HALO + length] * vec[0:1]
    for k in range(1, TAPS):
        filtered = filtered + rows[HALO - k : HALO - k + length] * same[0, :, k : k + 1] * vec[k : k + 1]
    conv[0] = filtered
    r_gate = jax.nn.sigmoid(split_dot(filtered, gates[0]) + vec[5:6])
    i_gate = jax.nn.sigmoid(split_dot(filtered, gates[1]) + vec[6:7])
    rate[0] = r_gate
    gate_in[0] = i_gate
    decay, square = decay_terms(r_gate, vec[7:8])
    a = decay * same[0, :, 1:2]
    b = jnp.sqrt(square) * i_gate * filtered
    width = a.shape[1]
    tiles = length // 8
    a = a.reshape(tiles, 8, width)
    b = b.reshape(tiles, 8, width)
    row = lax.broadcasted_iota(jnp.int32, (tiles, 8, width), 1)
    for d in (1, 2, 4):
        a_back = jnp.where(row >= d, pltpu.roll(a, d, 1), 1.0)
        b_back = jnp.where(row >= d, pltpu.roll(b, d, 1), 0.0)
        b = b + a * b_back
        a = a * a_back
    keep_a[...] = a.reshape(length, width)
    keep_b[...] = b.reshape(length, width)
    carry_s = jnp.zeros((1, width), F32)
    carry_a = jnp.ones((1, width), F32)
    for t in range(tiles):
        at = keep_a[t * 8 : t * 8 + 8]
        bt = keep_b[t * 8 : t * 8 + 8]
        s = bt + at * carry_s
        p = at * carry_a
        at_row = (t * 8) % step
        state[0, order[t * 8 // step], at_row : at_row + 8] = s
        prods[0, order[t * 8 // step], at_row : at_row + 8] = p
        carry_s = s[7:8]
        carry_a = p[7:8]
    ends[0, 0:1] = carry_a
    ends[0, 1:2] = carry_s
    ends[0, 2:8] = jnp.zeros((6, width), F32)


def reverse_kernel(order, d_state, same, vec, rate, grads, prods, ends, keep_g, keep_a):
    nx, step = d_state.shape[1], d_state.shape[2]
    length = nx * step
    width = rate.shape[2]
    decay, _ = decay_terms(rate[0], vec[7:8])
    a = decay * same[0, :, 1:2]
    keep_a[0:length] = a
    keep_a[length : length + 8] = jnp.ones((8, width), F32)
    for i in range(nx):
        keep_g[i * step : (i + 1) * step] = d_state[0, order[i]].astype(F32)
    first = a[0:1]
    tiles = length // 8
    nxt = keep_a[1 : length + 1].reshape(tiles, 8, width)
    g = keep_g[...].reshape(tiles, 8, width)
    row = lax.broadcasted_iota(jnp.int32, (tiles, 8, width), 1)
    p = nxt
    for d in (1, 2, 4):
        g_ahead = jnp.where(row < 8 - d, pltpu.roll(g, 8 - d, 1), 0.0)
        p_ahead = jnp.where(row < 8 - d, pltpu.roll(p, 8 - d, 1), 1.0)
        g = g + p * g_ahead
        p = p * p_ahead
    keep_g[...] = g.reshape(length, width)
    keep_a[0:length] = p.reshape(length, width)
    carry_g = jnp.zeros((1, width), F32)
    carry_p = jnp.ones((1, width), F32)
    for t in reversed(range(tiles)):
        pt = keep_a[t * 8 : t * 8 + 8]
        gt = keep_g[t * 8 : t * 8 + 8] + pt * carry_g
        pt = pt * carry_p
        grads[0, t * 8 : t * 8 + 8] = gt
        prods[0, t * 8 : t * 8 + 8] = pt
        carry_g = gt[0:1]
        carry_p = pt[0:1]
    ends[0, 0:1] = first * carry_p
    ends[0, 1:2] = first * carry_g
    ends[0, 2:8] = jnp.zeros((6, width), F32)


def final_kernel(
    order, u, halo, same, vec, gates, conv, rate, gate_in, state, prods, start, grads, back, carry,
    d_u, head, d_rate, d_input, sums, rows, tail,
):
    nx, step = u.shape[1], u.shape[2]
    length = nx * step
    width = conv.shape[2]
    d_s = grads[0] + back[0] * carry[0, 0:1]
    for i in range(nx):
        rows[HALO + i * step : HALO + (i + 1) * step] = (
            state[0, order[i]] + prods[0, order[i]] * start[0, 0:1]
        )
    rows[HALO - 1 : HALO] = start[0, 0:1]
    s_prev = rows[HALO - 1 : HALO - 1 + length]
    r_gate, i_gate, filtered = rate[0], gate_in[0], conv[0]
    decay, square = decay_terms(r_gate, vec[7:8])
    inverse = lax.rsqrt(jnp.maximum(square, 1e-37))
    scale = square * inverse
    a = decay * same[0, :, 1:2]
    d_scaled = d_s * i_gate * filtered
    d_log = d_s * s_prev * a - d_scaled * (decay * decay) * inverse
    d_i = d_s * scale * filtered * i_gate * (1.0 - i_gate)
    d_r = d_log * vec[7:8] * r_gate * (1.0 - r_gate)
    d_r_low = d_r.astype(BF16)
    d_i_low = d_i.astype(BF16)
    d_rate[0] = d_r_low
    d_input[0] = d_i_low
    back_dims = (((1,), (1,)), ((), ()))
    d_c = (
        d_s * scale * i_gate
        + lax.dot_general(d_r_low, gates[0], back_dims, preferred_element_type=F32)
        + lax.dot_general(d_i_low, gates[1], back_dims, preferred_element_type=F32)
    )
    rows[0:HALO] = halo[0]
    for i in range(nx):
        rows[HALO + i * step : HALO + (i + 1) * step] = u[0, order[i]].astype(F32)

    def column(value):
        return jnp.sum(value, axis=0, keepdims=True)

    parts = [column(d_c * rows[HALO : HALO + length])]
    tail[0:HALO] = jnp.zeros((HALO, width), F32)
    tail[HALO + length : 2 * HALO + length] = jnp.zeros((HALO, width), F32)
    d_rows = d_c * vec[0:1]
    d_head = jnp.zeros((HALO, width), F32)
    for k in range(1, TAPS):
        masked = d_c * same[0, :, k : k + 1]
        parts.append(column(masked * rows[HALO - k : HALO - k + length]))
        tail[HALO : HALO + length] = masked * vec[k : k + 1]
        d_rows = d_rows + tail[HALO + k : HALO + k + length]
        d_head = d_head + tail[k : k + HALO]
    for i in range(nx):
        d_u[0, order[i]] = d_rows[i * step : (i + 1) * step]
    head[0] = d_head
    parts += [column(d_c), column(d_r), column(d_i), column(d_log * r_gate)]

    @pl.when(pl.program_id(0) == 0)
    def _():
        sums[...] = jnp.zeros_like(sums)

    for i, value in enumerate(parts):
        sums[i : i + 1] += value


def chain_spec(*dims):
    return pl.BlockSpec((1, *dims), lambda i: (i,) + (0,) * len(dims))


def whole_spec(*dims):
    return pl.BlockSpec(dims, lambda i: (0,) * len(dims))


def scan_call(kernel, chains, operands, outs, scratch, flops):
    specs = [pl.BlockSpec(memory_space=pltpu.SMEM)]
    for value, chained in operands[1:]:
        specs.append(chain_spec(*value.shape[1:]) if chained else whole_spec(*value.shape))
    shapes, out_specs = [], []
    for shape, dtype, chained in outs:
        shapes.append(jax.ShapeDtypeStruct(shape, dtype))
        out_specs.append(chain_spec(*shape[1:]) if chained else whole_spec(*shape))
    moved = sum(v.size * v.dtype.itemsize for v, _ in operands)
    moved += sum(s.size * s.dtype.itemsize for s in shapes)
    return pl.pallas_call(
        kernel,
        grid=(chains,),
        in_specs=specs,
        out_specs=out_specs,
        out_shape=shapes,
        scratch_shapes=[pltpu.VMEM(s, F32) for s in scratch],
        compiler_params=pltpu.CompilerParams(vmem_limit_bytes=48 * 1024 * 1024),
        cost_estimate=pl.CostEstimate(flops=flops, bytes_accessed=moved, transcendentals=0),
    )(*[v for v, _ in operands])


def norm_back(weighted, rows_in, scale_vec):
    return scale_vec * weighted - rows_in * scale_vec**3 * jnp.mean(
        weighted * rows_in, axis=-1, keepdims=True
    )


def mix(left, right):
    return jnp.dot(left, right, preferred_element_type=F32)


def mix_back(left, right):
    return lax.dot_general(left, right, (((1,), (1,)), ((), ())), preferred_element_type=F32)


def on_device(
    grid,
    inputs,
    seg_ids,
    norm_in,
    proj_y,
    proj_x,
    conv_weight,
    conv_bias,
    rate_weight,
    rate_bias,
    input_weight,
    input_bias,
    decay_param,
    proj_out,
    norm_mlp,
    mlp_gate,
    mlp_up,
    mlp_down,
    cotangent,
):
    nx, ny, nz, nc = (grid.n[p] for p in "xyzc")
    x, y, z, c = (grid.index(p) for p in "xyzc")
    micro, step, depth = inputs.shape
    chains = micro * ny
    length = nx * step
    shard = proj_x.shape[0]

    gain_in = norm_in.astype(F32)[:, None]
    gain_mlp = norm_mlp.astype(F32)[:, None]

    def gained(matrix, gain):
        return (matrix.astype(F32) * gain).astype(BF16)

    width = proj_x.shape[1] // (nx * ny)
    ff_width = mlp_down.shape[1] // (nx * ny)
    plane = nx * ny * shard
    width = proj_x.shape[1] // (nx * ny)
    ff_width = mlp_down.shape[1] // (nx * ny)
    plane = nx * ny * shard
    slope = -8.0 * jax.nn.softplus(-decay_param)
    slope_back = 8.0 * jax.nn.sigmoid(-decay_param)
    small = jnp.concatenate(
        [conv_weight, conv_bias[None], rate_bias[None], input_bias[None], slope[None]], axis=0
    )
    share = small.shape[1]
    heads, block = rate_weight.shape[0], rate_weight.shape[1]
    per = nz // ny
    packed = pack_small(rate_weight, input_weight, small)
    beside = [grid.shift(seg_ids, "y", r) for r in range(1, ny)]
    weights_in = grid.columns_of(
        [gained(proj_x, gain_in), gained(proj_y, gain_in), proj_out]
    ).reshape(plane, 3 * width)
    own_rows = grid.turn(after(inputs, weights_in))
    source = own_rows.astype(F32)
    normed, in_hop = grid.spread(own_rows, normed=True)
    own_x, own_yo = weights_in[:, :width], weights_in[:, width:]
    first_x = grid.ring_first(own_x)
    half = lax.dynamic_index_in_dim(after(packed, weights_in), c, 0, keepdims=False)
    by_z = grid.place([half] + [grid.shift(half, "z", r) for r in range(1, nz)], "z")
    by_z = lax.dynamic_slice_in_dim(by_z, y * per, per, 0)
    blocks_x = grid.ring_rest(own_x, first_x, by_z, *in_hop)
    (mix_x,) = grid.whole_rows(blocks_x, 0)
    first_yo = grid.ring_first(after(own_yo, *blocks_x))
    by_x = grid.place([by_z] + [grid.shift(by_z, "x", r) for r in range(1, nx)], "x")
    by_x = jnp.moveaxis(by_x, 0, 1).reshape(per * nx, *half.shape)
    halves = grid.place([by_x] + [grid.shift(by_x, "c", r) for r in range(1, nc)], "c")
    pieces = [gained(mlp_gate, gain_mlp), gained(mlp_up, gain_mlp), mlp_down]
    weights_ff = grid.columns_of([after(p, weights_in) for p in pieces]).reshape(plane, -1)

    drive = mix(normed, mix_x).astype(BF16).reshape(chains, nx, step, width)
    own_cot = grid.turn(after(cotangent, drive))
    gates, vec = unpack_small(after(halves, drive), x, per, heads)
    segments = after(jnp.stack([seg_ids, *beside], axis=1), drive)
    padded = jnp.pad(segments, ((0, 0), (0, 0), (HALO, 0)), constant_values=-1)
    near = lax.dynamic_slice_in_dim(padded, z * length, length + HALO, 2)
    here = near[:, :, HALO:]
    same = [jnp.ones_like(here, dtype=F32)]
    for k in range(1, TAPS):
        same.append((near[:, :, HALO - k : HALO - k + length] == here).astype(F32))
    same = jnp.stack(same + [jnp.zeros_like(same[0])] * (8 - TAPS), axis=-1)
    same = same.reshape(chains, length, 8)
    order = ((x - jnp.arange(nx, dtype=jnp.int32)) % nx).astype(jnp.int32)

    blocks_yo = grid.ring_rest(own_yo, first_yo, drive)
    ff_all = grid.all_rows(after(weights_ff, *blocks_yo))
    mix_y, mix_out = grid.whole_rows(blocks_yo, 0, 1)
    pre_y = mix(normed, mix_y)
    branch_y, gelu_y_back = jax.vjp(jax.nn.gelu, pre_y)
    last = lax.dynamic_index_in_dim(drive, (x - (nx - 1)) % nx, 1, keepdims=False)
    halo = grid.shift(last[:, step - HALO :].astype(F32), "z", 1, wrap=False)
    shape = (chains, length, width)
    turned = (chains, nx, step, width)
    conv, rate, gate_in, state, prods, ends = scan_call(
        forward_kernel,
        chains,
        [(order, False), (drive, True), (halo, True), (same, True), (vec, False), (gates, False)],
        [(shape, F32, True)] * 3 + [(turned, F32, True)] * 2 + [((chains, 8, width), F32, True)],
        [(length + HALO, width), (length, width), (length, width)],
        flops=8 * chains * length * width * width,
    )

    def carry_from(summary, sign):
        carry = jnp.zeros((chains, 1, width), F32)
        for r in reversed(range(1, nz)):
            got = grid.shift(summary, "z", sign * r, wrap=False)
            carry = got[:, 1:2] + got[:, 0:1] * carry
        return carry

    rows_cot, cot_hop = grid.spread(own_cot, ends)
    start = carry_from(after(ends, *cot_hop)[:, 0:2], 1)
    hidden = (state + prods * start[:, None]).astype(BF16)
    hidden_f = hidden.reshape(chains * length, width).astype(F32)
    mixed = (branch_y * hidden_f).astype(BF16)
    resid = source + grid.collect(mix_back(mixed, mix_out).astype(BF16), micro)

    scale_mlp = lax.rsqrt(jnp.mean(resid * resid, axis=-1, keepdims=True) + NORM_EPS)
    normed_mlp, _ = grid.spread((resid * scale_mlp).astype(BF16))
    ff_all = after(ff_all, normed_mlp)
    ff_gate = ff_all[:, :ff_width]
    ff_up = ff_all[:, ff_width : 2 * ff_width]
    ff_down = ff_all[:, 2 * ff_width :]
    pre_gate = mix(normed_mlp, ff_gate)
    pre_up = mix(normed_mlp, ff_up)
    activated, gelu_gate_back = jax.vjp(jax.nn.gelu, pre_gate)
    product = (activated * pre_up).astype(BF16)
    grad_prod = mix(rows_cot, ff_down)
    grad_gate = gelu_gate_back(grad_prod * pre_up)[0].astype(BF16)
    grad_up = (grad_prod * activated).astype(BF16)
    part_mlp = (mix_back(grad_gate, ff_gate) + mix_back(grad_up, ff_up)).astype(BF16)
    weighted_mlp = grid.collect(part_mlp, micro)
    grad_ff = jnp.concatenate([grad_gate, grad_up], axis=1)
    sum_down = WeightSum(grid, rows_cot, after(product, part_mlp))
    sum_ff = WeightSum(grid, normed_mlp, after(grad_ff, part_mlp))
    sum_down.meet()
    sum_ff.meet()
    sum_ff.mine = jnp.concatenate([sum_ff.mine.astype(BF16), sum_down.mine.astype(BF16)], axis=1)
    sum_ff.along_z()
    grad_resid = own_cot.astype(F32) + norm_back(weighted_mlp, resid, scale_mlp)
    grad_branch, _ = grid.spread(grad_resid.astype(BF16), sum_ff.mine)

    grad_mixed = mix(grad_branch, mix_out)
    grad_pre_y = gelu_y_back(grad_mixed * hidden_f)[0].astype(BF16)
    grad_state = (grad_mixed * branch_y).astype(BF16).reshape(turned)
    d_local, d_prods, d_ends = scan_call(
        reverse_kernel,
        chains,
        [(order, False), (grad_state, True), (same, True), (vec, False), (rate, True)],
        [(shape, F32, True)] * 2 + [((chains, 8, width), F32, True)],
        [(length, width), (length + HALO, width)],
        flops=40 * chains * length * width,
    )
    d_carry = carry_from(d_ends[:, 0:2], -1)
    d_drive, head, *d_pre, sums = scan_call(
        final_kernel,
        chains,
        [
            (order, False),
            (drive, True),
            (halo, True),
            (same, True),
            (vec, False),
            (gates, False),
            (conv, True),
            (rate, True),
            (gate_in, True),
            (state, True),
            (prods, True),
            (start, True),
            (d_local, True),
            (d_prods, True),
            (d_carry, True),
        ],
        [
            (turned, F32, True),
            ((chains, HALO, width), F32, True),
            (shape, BF16, True),
            (shape, BF16, True),
            ((8, width), F32, False),
        ],
        [(length + HALO, width), (length + 2 * HALO, width)],
        flops=8 * chains * length * width * width,
    )
    behind = grid.shift(head, "z", -1, wrap=False)
    chunk = lax.broadcasted_iota(jnp.int32, (1, nx, 1, 1), 1)
    tail = jnp.pad(behind, ((0, 0), (step - HALO, 0), (0, 0)))[:, None]
    d_drive = d_drive + jnp.where(chunk == (x - (nx - 1)) % nx, tail, 0.0)
    grad_drive = d_drive.astype(BF16).reshape(chains * length, width)
    part_in = (mix_back(grad_pre_y, mix_y) + mix_back(grad_drive, mix_x)).astype(BF16)
    weighted_in = grid.collect(part_in, micro)
    both = jnp.concatenate([grad_pre_y, grad_drive], axis=1)
    sum_in = WeightSum(grid, normed, after(both, weighted_in))
    sum_out = WeightSum(grid, grad_branch, after(mixed, weighted_in))
    sum_in.meet()
    sum_out.meet()
    sum_in.mine = jnp.concatenate([sum_in.mine.astype(BF16), sum_out.mine.astype(BF16)], axis=1)
    sum_in.along_z(sum_ff.done)
    part_out = mix_back(after(product, weighted_in), ff_down).astype(BF16)
    block_out = resid + grid.collect(part_out, micro)
    block_out = grid.turn(block_out.astype(BF16), back=True)
    grad_gate_w, grad_up_w, grad_down_w = sum_ff.finish(3)
    grad_y_w, grad_x_w, grad_out_w = sum_in.finish(3)
    scale_in = lax.rsqrt(jnp.mean(source * source, axis=-1, keepdims=True) + NORM_EPS)
    grad_source = grad_resid + norm_back(weighted_in, source, scale_in)
    grad_source = grid.turn(grad_source.astype(BF16), back=True)

    def gain_grad(*pairs):
        return sum(jnp.sum(w.astype(F32) * g, axis=1) for w, g in pairs)

    grad_norm_in = gain_grad((proj_y, grad_y_w), (proj_x, grad_x_w))
    grad_norm_mlp = gain_grad((mlp_gate, grad_gate_w), (mlp_up, grad_up_w))

    d_pre = [after(v, weighted_in) for v in d_pre]
    conv_low = conv.reshape(chains * length, width).astype(BF16)
    gate_dense = [
        lax.dot_general(
            conv_low,
            d.reshape(chains * length, width),
            (((0,), (0,)), ((), ())),
            preferred_element_type=F32,
        )
        for d in d_pre
    ]
    blocks = jnp.stack(
        [
            jnp.concatenate(
                [d[h * block : (h + 1) * block, h * block : (h + 1) * block] for d in gate_dense]
                + [sums[:, h * block : (h + 1) * block]],
                axis=0,
            )
            for h in range(per * heads)
        ]
    )
    blocks = blocks.astype(BF16).reshape(per, heads, 2 * block + 8, block)
    blocks = grid.total(blocks, "c")
    blocks = grid.total(blocks, "z")
    got = [
        [grid.shift_plane(blocks, ry, rx) if ry or rx else blocks for rx in range(nx)]
        for ry in range(ny)
    ]
    by_y = grid.place([grid.place(row, "x") for row in got], "y")
    mine = lax.dynamic_index_in_dim(
        by_y.reshape(ny * nx * per, *blocks.shape[1:]), z * nx + x, 0, keepdims=False
    ).astype(F32)
    mats = mine[:, : 2 * block].reshape(heads, 2, block, block)
    sums_own = jnp.moveaxis(mine[:, 2 * block :], 0, 1).reshape(8, share)
    return (
        block_out,
        grad_source,
        grad_norm_in,
        grad_y_w * gain_in,
        grad_x_w * gain_in,
        sums_own[0:4],
        sums_own[4],
        mats[:, 0],
        sums_own[5],
        mats[:, 1],
        sums_own[6],
        sums_own[7] * slope_back,
        grad_out_w,
        grad_norm_mlp,
        grad_gate_w * gain_mlp,
        grad_up_w * gain_mlp,
        grad_down_w,
    )


def solution(mesh):
    grid = Grid(mesh.shape["seq"], mesh.shape["blk"])
    every = ("seq", "blk")
    placed = (
        P(None, every, None),
        P(None, "seq"),
        P(every),
        P(every, None),
        P(every, None),
        P(None, "blk"),
        P("blk"),
        P("blk", None, None),
        P("blk"),
        P("blk", None, None),
        P("blk"),
        P("blk"),
        P(every, None),
        P(every),
        P(every, None),
        P(every, None),
        P(every, None),
        P(None, every, None),
    )
    return jax.shard_map(
        functools.partial(on_device, grid),
        mesh=mesh,
        in_specs=placed,
        out_specs=(
            P(None, every, None),
            P(None, every, None),
            P(every),
            P(every, None),
            P(every, None),
            P(None, "blk"),
            P("blk"),
            P("blk", None, None),
            P("blk"),
            P("blk", None, None),
            P("blk"),
            P("blk"),
            P(every, None),
            P(every),
            P(every, None),
            P(every, None),
            P(every, None),
        ),
        check_vma=False,
    )
```

```python
import functools

import jax
import jax.numpy as jnp
from jax import lax
from jax.experimental import pallas as pl
from jax.experimental.pallas import tpu as pltpu
from jax.sharding import PartitionSpec as P

NORM_EPS = 1e-06
F32 = jnp.float32
BF16 = jnp.bfloat16
TAPS = 4
HALO = 8


class Grid:
    def __init__(self, n_seq, n_blk):
        core = 2 if n_seq % 2 == 0 else 1
        nx = max(d for d in range(1, n_blk + 1) if d * d <= n_blk and n_blk % d == 0)
        self.n = {"y": n_seq // core, "c": core, "z": n_blk // nx, "x": nx}
        self.n_blk = n_blk

    def index(self, part):
        seq, blk = lax.axis_index("seq"), lax.axis_index("blk")
        return {
            "y": seq // self.n["c"],
            "c": seq % self.n["c"],
            "z": blk // self.n["x"],
            "x": blk % self.n["x"],
        }[part]

    def shift(self, value, part, by, wrap=True):
        outer, inner, axis = {
            "y": ("y", "c", "seq"),
            "c": ("y", "c", "seq"),
            "z": ("z", "x", "blk"),
            "x": ("z", "x", "blk"),
        }[part]
        pairs = []
        for o in range(self.n[outer]):
            for i in range(self.n[inner]):
                p = (o if part == outer else i) + by
                if not wrap and not 0 <= p < self.n[part]:
                    continue
                p = p % self.n[part]
                to = (p, i) if part == outer else (o, p)
                pairs.append((o * self.n[inner] + i, to[0] * self.n[inner] + to[1]))
        return lax.ppermute(value, axis, pairs)

    def shift_plane(self, value, by_y, by_x):
        ny, nc, nz, nx = (self.n[p] for p in "yczx")
        pairs = []
        for y in range(ny):
            for c in range(nc):
                for z in range(nz):
                    for x in range(nx):
                        to = (((y + by_y) % ny * nc + c) * nz + z) * nx + (x + by_x) % nx
                        pairs.append((((y * nc + c) * nz + z) * nx + x, to))
        return lax.ppermute(value, ("seq", "blk"), pairs)

    def rows_ahead(self, rows):
        ny, nc, nz, nx = (self.n[p] for p in "yczx")
        out = None
        for x in range(nx):
            pairs = []
            for s in range(ny * nc):
                for z in range(nz - 1):
                    pairs.append(((s * nz + z) * nx + nx - 1, (s * nz + z + 1) * nx + x))
            got = lax.ppermute(rows, ("seq", "blk"), pairs)
            out = got if out is None else out + got
        return out

    def place(self, by_shift, part):
        n, me = self.n[part], self.index(part)
        if n == 1:
            return by_shift[0][None]
        if n == 2:
            here, there = by_shift
            low = me == 0
            return jnp.stack([jnp.where(low, here, there), jnp.where(low, there, here)])
        out = jnp.zeros((n, *by_shift[0].shape), by_shift[0].dtype)
        for r, value in enumerate(by_shift):
            out = lax.dynamic_update_index_in_dim(out, value, (me - r) % n, 0)
        return out

    def gather(self, value, part):
        n = self.n[part]
        return self.place([value] + [self.shift(value, part, r) for r in range(1, n)], part)

    def exchange(self, value, part, dim):
        n, me = self.n[part], self.index(part)
        got = []
        for r in range(n):
            piece = lax.dynamic_index_in_dim(value, (me + r) % n, dim, keepdims=False)
            got.append(self.shift(piece, part, r) if r else piece)
        return self.place(got, part)

    def total(self, value, part, *late):
        out = value.astype(F32)
        for r in range(1, self.n[part]):
            out = out + after(self.shift(value, part, r), *late).astype(F32)
        return out.astype(value.dtype)

    def turn(self, value, back=False):
        ny, nc, nz = self.n["y"], self.n["c"], self.n["z"]
        places = [
            (y * nc + c) * nz + z for c in range(nc) for z in range(nz) for y in range(ny)
        ]
        width = value.shape[-1] // len(places)
        if width % 128:
            cut = value.reshape(*value.shape[:-1], *((nc, nz, ny) if back else (ny, nc, nz)), width)
            k = value.ndim - 1
            order = (k + 2, k, k + 1) if back else (k + 1, k + 2, k)
            return cut.transpose(tuple(range(k)) + order + (k + 3,)).reshape(value.shape)

        def kernel(src, dst):
            for k, place in enumerate(places):
                here, there = pl.ds(k * width, width), pl.ds(place * width, width)
                if back:
                    dst[:, :, there] = src[:, :, here]
                else:
                    dst[:, :, here] = src[:, :, there]

        return pl.pallas_call(
            kernel,
            out_shape=jax.ShapeDtypeStruct(value.shape, value.dtype),
            cost_estimate=pl.CostEstimate(flops=0, bytes_accessed=4 * value.size, transcendentals=0),
        )(value)

    def spread(self, shard, *late, normed=False):
        nx, ny = self.n["x"], self.n["y"]
        micro, step, width = shard.shape
        got = {(0, 0): shard}
        for r in range(1, nx):
            got[0, r] = after(self.shift(shard, "x", r), *late)
        for r in range(1, ny):
            got[r, 0] = after(self.shift(shard, "y", r), *late)
        hop = [v for k, v in got.items() if k != (0, 0)]
        out = []
        for m in range(micro):
            for ry in range(ny):
                for rx in range(nx):
                    if ry == 0 or rx == 0:
                        out.append((got[ry, rx], m))
                    elif m % 2 == 0:
                        out.append((self.shift(got[0, rx][m], "y", ry), None))
                    else:
                        out.append((self.shift(got[ry, 0][m], "x", rx), None))
        rows = assemble_rows(out, step, width, normed)
        return rows.reshape(len(out) * step, width), hop

    def collect(self, partial, micro, *late):
        nx, ny = self.n["x"], self.n["y"]
        part = partial.reshape(micro, ny, nx, -1, partial.shape[1])
        out = []
        for m in range(micro):
            if m % 2 == 0:
                held = part[m, 0].astype(F32)
                for r in range(1, ny):
                    held = held + after(self.shift(part[m, r], "y", -r), *late).astype(F32)
                last, n = "x", nx
            else:
                held = part[m, :, 0].astype(F32)
                for r in range(1, nx):
                    held = held + after(self.shift(part[m, :, r], "x", -r), *late).astype(F32)
                last, n = "y", ny
            total = held[0]
            for r in range(1, n):
                total = total + self.shift(held[r].astype(BF16), last, -r).astype(F32)
            out.append(total)
        return jnp.stack(out)

    def columns_of(self, pieces, *late):
        nx, ny = self.n["x"], self.n["y"]
        x, y = self.index("x"), self.index("y")

        def take(yy, xx):
            out = []
            for w in pieces:
                width = w.shape[1] // (nx * ny)
                out.append(lax.dynamic_slice_in_dim(w, (yy * nx + xx) * width, width, 1))
            return out[0] if len(out) == 1 else jnp.concatenate(out, axis=1)

        rows = []
        for ry in range(ny):
            got = []
            for rx in range(nx):
                piece = take((y + ry) % ny, (x + rx) % nx)
                got.append(after(self.shift_plane(piece, ry, rx), *late) if ry or rx else piece)
            rows.append(self.place(got, "x"))
        return self.place(rows, "y")

    def z_groups(self):
        nz, nx = self.n["z"], self.n["x"]
        return [[z * nx + x for z in range(nz)] for x in range(nx)]

    def all_rows(self, block):
        ny, nc, nz, nx = (self.n[p] for p in "yczx")
        groups = [
            [((y * nc + c) * nz + z) * nx + x for c in range(nc) for z in range(nz)]
            for y in range(ny)
            for x in range(nx)
        ]
        return lax.all_gather(
            block, ("seq", "blk"), axis=0, tiled=True, axis_index_groups=groups
        )

    def to_owners(self, done, *late):
        nx, ny = self.n["x"], self.n["y"]
        x, y = self.index("x"), self.index("y")
        rows = []
        for ry in range(ny):
            got = []
            for rx in range(nx):
                piece = lax.dynamic_slice(
                    done, ((y + ry) % ny, (x + rx) % nx, 0, 0), (1, 1, *done.shape[2:])
                )[0, 0]
                got.append(after(self.shift_plane(piece, ry, rx), *late) if ry or rx else piece)
            rows.append(self.place(got, "x"))
        return self.place(rows, "y")


class WeightSum:
    def __init__(self, grid, left, right):
        self.grid, self.left, self.right = grid, left, right
        self.share = left.shape[1] // grid.n["c"]

    def product(self, core):
        cut = lax.dynamic_slice_in_dim(self.left, core * self.share, self.share, 1)
        return lax.dot_general(
            cut, self.right, (((0,), (0,)), ((), ())), preferred_element_type=F32
        )

    def lend(self):
        nc, c = self.grid.n["c"], self.grid.index("c")
        self.lent = [self.product((c + s) % nc).astype(BF16) for s in range(1, nc)]

    def meet(self):
        mine = self.product(self.grid.index("c"))
        for s, lent in enumerate(self.lent):
            mine = mine + self.grid.shift(lent, "c", s + 1).astype(F32)
        self.mine = mine

    def along_z(self, *late):
        self.done = lax.psum_scatter(
            after(self.mine.astype(BF16), *late),
            "blk",
            scatter_dimension=0,
            tiled=True,
            axis_index_groups=self.grid.z_groups(),
        )

    def finish(self, count, *late):
        grid = self.grid
        ny, nx = grid.n["y"], grid.n["x"]
        width = self.done.shape[1] // count
        done = after(self.done, *late).reshape(ny, nx, -1, self.done.shape[1])
        side = grid.to_owners(done)
        return [
            jnp.concatenate(
                [
                    side[yy, xx, :, i * width : (i + 1) * width].astype(F32)
                    for yy in range(ny)
                    for xx in range(nx)
                ],
                axis=1,
            )
            for i in range(count)
        ]


def after(value, *others):
    return lax.optimization_barrier((value, *others))[0]


def assemble_rows(pieces, step, width, normed):
    arrays = []
    for value, _ in pieces:
        if not any(value is a for a in arrays):
            arrays.append(value)
    which = [next(i for i, a in enumerate(arrays) if a is value) for value, _ in pieces]
    cut = 32 if step % 32 == 0 else step

    def kernel(*refs):
        out = refs[-1]
        for k, (_, lead) in enumerate(pieces):
            ref = refs[which[k]]
            block = ref[...] if lead is None else ref[lead]
            if normed:
                block = block.astype(F32)
                square = jnp.mean(block * block, axis=-1, keepdims=True)
                block = (block * lax.rsqrt(square + NORM_EPS)).astype(out.dtype)
            out[k] = block

    specs = []
    for a in arrays:
        if a.ndim == 2:
            specs.append(pl.BlockSpec((cut, width), lambda i: (i, 0)))
        else:
            specs.append(pl.BlockSpec((a.shape[0], cut, width), lambda i: (0, i, 0)))
    count = len(pieces)
    return pl.pallas_call(
        kernel,
        grid=(step // cut,),
        in_specs=specs,
        out_specs=pl.BlockSpec((count, cut, width), lambda i: (0, i, 0)),
        out_shape=jax.ShapeDtypeStruct((count, step, width), BF16),
        compiler_params=pltpu.CompilerParams(vmem_limit_bytes=32 * 1024 * 1024),
        cost_estimate=pl.CostEstimate(
            flops=0, bytes_accessed=4 * count * step * width, transcendentals=0
        ),
    )(*arrays)


def pack_small(rate_weight, input_weight, small):
    heads, block, _ = rate_weight.shape
    rows = heads * block
    by_head = jnp.moveaxis(small.reshape(8, heads, block), 1, 0)
    by_head = jnp.pad(by_head, ((0, 0), (0, 8), (0, 0))).reshape(heads * 16, block)

    def kernel(rate, gate_in, values, out):
        for h in range(heads):
            out[0, h * block : (h + 1) * block] = rate[h]
            out[1, h * block : (h + 1) * block] = gate_in[h]
        rest = values[...]
        for t in range(3):
            high = rest.astype(BF16)
            at = rows + t * heads * 16
            out[0, at : at + heads * 16] = high
            out[1, at : at + heads * 16] = high
            rest = rest - high.astype(F32)

    return pl.pallas_call(
        kernel,
        out_shape=jax.ShapeDtypeStruct((2, rows + 48 * heads, block), BF16),
        cost_estimate=pl.CostEstimate(flops=0, bytes_accessed=8 * rows * block, transcendentals=0),
    )(rate_weight, input_weight, by_head)


def unpack_small(halves, place, per, heads):
    _, _, depth, block = halves.shape
    rows = heads * block
    width = per * rows

    def kernel(which, share, gates, vec):
        row = lax.broadcasted_iota(jnp.int32, (block, width), 0)
        column = lax.broadcasted_iota(jnp.int32, (block, width), 1)
        total = jnp.zeros((16, width), F32)
        for p in range(per):
            for h in range(heads):
                head = p * heads + h
                pick = jnp.where(column == row + head * block, 1.0, 0.0).astype(BF16)
                for g in range(2):
                    part = share[g, p, h * block : (h + 1) * block]
                    gates[g, head * block : (head + 1) * block] = jnp.dot(
                        part, pick, preferred_element_type=F32
                    ).astype(BF16)
                for t in range(3):
                    at = rows + (t * heads + h) * 16
                    total = total + jnp.dot(
                        share[0, p, at : at + 16], pick, preferred_element_type=F32
                    )
        vec[...] = total[0:8]

    return pl.pallas_call(
        kernel,
        grid_spec=pltpu.PrefetchScalarGridSpec(
            num_scalar_prefetch=1,
            grid=(1,),
            in_specs=[pl.BlockSpec((2, per, depth, block), lambda i, which: (0, which[0], 0, 0))],
            out_specs=[
                pl.BlockSpec((2, width, width), lambda i, which: (0, 0, 0)),
                pl.BlockSpec((8, width), lambda i, which: (0, 0)),
            ],
        ),
        out_shape=[
            jax.ShapeDtypeStruct((2, width, width), BF16),
            jax.ShapeDtypeStruct((8, width), F32),
        ],
        compiler_params=pltpu.CompilerParams(vmem_limit_bytes=32 * 1024 * 1024),
        cost_estimate=pl.CostEstimate(
            flops=0, bytes_accessed=4 * width * width, transcendentals=0
        ),
    )(place.astype(jnp.int32)[None], halves)


def decay_terms(rate, slope):
    log_decay = rate * slope
    small = 1.0 / 40320.0
    for div in (5040.0, 720.0, 120.0, 24.0, 6.0, 2.0, 1.0):
        small = small * log_decay + 1.0 / div
    less = jnp.where(log_decay < -0.4, jnp.exp(log_decay) - 1.0, log_decay * small)
    decay = 1.0 + less
    square = -less * (1.0 + decay)
    return decay, square


def split_dot(value, weight):
    high = value.astype(BF16)
    rest = (value - high.astype(F32)).astype(BF16)
    return jnp.dot(high, weight, preferred_element_type=F32) + jnp.dot(
        rest, weight, preferred_element_type=F32
    )


def forward_kernel(order, u, halo, same, vec, gates, conv, rate, gate_in, state, prods, ends, rows, keep_a, keep_b):
    nx, step = u.shape[1], u.shape[2]
    length = nx * step
    rows[0:HALO] = halo[0]
    for i in range(nx):
        rows[HALO + i * step : HALO + (i + 1) * step] = u[0, order[i]].astype(F32)
    filtered = vec[4:5] + rows[HALO : HALO + length] * vec[0:1]
    for k in range(1, TAPS):
        filtered = filtered + rows[HALO - k : HALO - k + length] * same[0, :, k : k + 1] * vec[k : k + 1]
    conv[0] = filtered
    r_gate = jax.nn.sigmoid(split_dot(filtered, gates[0]) + vec[5:6])
    i_gate = jax.nn.sigmoid(split_dot(filtered, gates[1]) + vec[6:7])
    rate[0] = r_gate
    gate_in[0] = i_gate
    decay, square = decay_terms(r_gate, vec[7:8])
    a = decay * same[0, :, 1:2]
    b = jnp.sqrt(square) * i_gate * filtered
    width = a.shape[1]
    tiles = length // 8
    a = a.reshape(tiles, 8, width)
    b = b.reshape(tiles, 8, width)
    row = lax.broadcasted_iota(jnp.int32, (tiles, 8, width), 1)
    for d in (1, 2, 4):
        a_back = jnp.where(row >= d, pltpu.roll(a, d, 1), 1.0)
        b_back = jnp.where(row >= d, pltpu.roll(b, d, 1), 0.0)
        b = b + a * b_back
        a = a * a_back
    keep_a[...] = a.reshape(length, width)
    keep_b[...] = b.reshape(length, width)
    carry_s = jnp.zeros((1, width), F32)
    carry_a = jnp.ones((1, width), F32)
    for t in range(tiles):
        at = keep_a[t * 8 : t * 8 + 8]
        bt = keep_b[t * 8 : t * 8 + 8]
        s = bt + at * carry_s
        p = at * carry_a
        at_row = (t * 8) % step
        state[0, order[t * 8 // step], at_row : at_row + 8] = s
        prods[0, order[t * 8 // step], at_row : at_row + 8] = p
        carry_s = s[7:8]
        carry_a = p[7:8]
    ends[0, 0:1] = carry_a
    ends[0, 1:2] = carry_s
    ends[0, 2:8] = jnp.zeros((6, width), F32)


def reverse_kernel(order, d_state, same, vec, rate, grads, prods, ends, keep_g, keep_a):
    nx, step = d_state.shape[1], d_state.shape[2]
    length = nx * step
    width = rate.shape[2]
    decay, _ = decay_terms(rate[0], vec[7:8])
    a = decay * same[0, :, 1:2]
    keep_a[0:length] = a
    keep_a[length : length + 8] = jnp.ones((8, width), F32)
    for i in range(nx):
        keep_g[i * step : (i + 1) * step] = d_state[0, order[i]].astype(F32)
    first = a[0:1]
    tiles = length // 8
    nxt = keep_a[1 : length + 1].reshape(tiles, 8, width)
    g = keep_g[...].reshape(tiles, 8, width)
    row = lax.broadcasted_iota(jnp.int32, (tiles, 8, width), 1)
    p = nxt
    for d in (1, 2, 4):
        g_ahead = jnp.where(row < 8 - d, pltpu.roll(g, 8 - d, 1), 0.0)
        p_ahead = jnp.where(row < 8 - d, pltpu.roll(p, 8 - d, 1), 1.0)
        g = g + p * g_ahead
        p = p * p_ahead
    keep_g[...] = g.reshape(length, width)
    keep_a[0:length] = p.reshape(length, width)
    carry_g = jnp.zeros((1, width), F32)
    carry_p = jnp.ones((1, width), F32)
    for t in reversed(range(tiles)):
        pt = keep_a[t * 8 : t * 8 + 8]
        gt = keep_g[t * 8 : t * 8 + 8] + pt * carry_g
        pt = pt * carry_p
        grads[0, t * 8 : t * 8 + 8] = gt
        prods[0, t * 8 : t * 8 + 8] = pt
        carry_g = gt[0:1]
        carry_p = pt[0:1]
    ends[0, 0:1] = first * carry_p
    ends[0, 1:2] = first * carry_g
    ends[0, 2:8] = jnp.zeros((6, width), F32)


def final_kernel(
    order, u, halo, same, vec, gates, conv, rate, gate_in, state, prods, start, grads, back, carry,
    d_u, head, d_rate, d_input, sums, rows, tail,
):
    nx, step = u.shape[1], u.shape[2]
    length = nx * step
    width = conv.shape[2]
    d_s = grads[0] + back[0] * carry[0, 0:1]
    for i in range(nx):
        rows[HALO + i * step : HALO + (i + 1) * step] = (
            state[0, order[i]] + prods[0, order[i]] * start[0, 0:1]
        )
    rows[HALO - 1 : HALO] = start[0, 0:1]
    s_prev = rows[HALO - 1 : HALO - 1 + length]
    r_gate, i_gate, filtered = rate[0], gate_in[0], conv[0]
    decay, square = decay_terms(r_gate, vec[7:8])
    inverse = lax.rsqrt(jnp.maximum(square, 1e-37))
    scale = square * inverse
    a = decay * same[0, :, 1:2]
    d_scaled = d_s * i_gate * filtered
    d_log = d_s * s_prev * a - d_scaled * (decay * decay) * inverse
    d_i = d_s * scale * filtered * i_gate * (1.0 - i_gate)
    d_r = d_log * vec[7:8] * r_gate * (1.0 - r_gate)
    d_r_low = d_r.astype(BF16)
    d_i_low = d_i.astype(BF16)
    d_rate[0] = d_r_low
    d_input[0] = d_i_low
    back_dims = (((1,), (1,)), ((), ()))
    d_c = (
        d_s * scale * i_gate
        + lax.dot_general(d_r_low, gates[0], back_dims, preferred_element_type=F32)
        + lax.dot_general(d_i_low, gates[1], back_dims, preferred_element_type=F32)
    )
    rows[0:HALO] = halo[0]
    for i in range(nx):
        rows[HALO + i * step : HALO + (i + 1) * step] = u[0, order[i]].astype(F32)

    def column(value):
        return jnp.sum(value, axis=0, keepdims=True)

    parts = [column(d_c * rows[HALO : HALO + length])]
    tail[0:HALO] = jnp.zeros((HALO, width), F32)
    tail[HALO + length : 2 * HALO + length] = jnp.zeros((HALO, width), F32)
    d_rows = d_c * vec[0:1]
    d_head = jnp.zeros((HALO, width), F32)
    for k in range(1, TAPS):
        masked = d_c * same[0, :, k : k + 1]
        parts.append(column(masked * rows[HALO - k : HALO - k + length]))
        tail[HALO : HALO + length] = masked * vec[k : k + 1]
        d_rows = d_rows + tail[HALO + k : HALO + k + length]
        d_head = d_head + tail[k : k + HALO]
    for i in range(nx):
        d_u[0, order[i]] = d_rows[i * step : (i + 1) * step]
    head[0] = d_head
    parts += [column(d_c), column(d_r), column(d_i), column(d_log * r_gate)]

    @pl.when(pl.program_id(0) == 0)
    def _():
        sums[...] = jnp.zeros_like(sums)

    for i, value in enumerate(parts):
        sums[i : i + 1] += value


def chain_spec(*dims):
    return pl.BlockSpec((1, *dims), lambda i: (i,) + (0,) * len(dims))


def whole_spec(*dims):
    return pl.BlockSpec(dims, lambda i: (0,) * len(dims))


def scan_call(kernel, chains, operands, outs, scratch, flops):
    specs = [pl.BlockSpec(memory_space=pltpu.SMEM)]
    for value, chained in operands[1:]:
        specs.append(chain_spec(*value.shape[1:]) if chained else whole_spec(*value.shape))
    shapes, out_specs = [], []
    for shape, dtype, chained in outs:
        shapes.append(jax.ShapeDtypeStruct(shape, dtype))
        out_specs.append(chain_spec(*shape[1:]) if chained else whole_spec(*shape))
    moved = sum(v.size * v.dtype.itemsize for v, _ in operands)
    moved += sum(s.size * s.dtype.itemsize for s in shapes)
    return pl.pallas_call(
        kernel,
        grid=(chains,),
        in_specs=specs,
        out_specs=out_specs,
        out_shape=shapes,
        scratch_shapes=[pltpu.VMEM(s, F32) for s in scratch],
        compiler_params=pltpu.CompilerParams(vmem_limit_bytes=48 * 1024 * 1024),
        cost_estimate=pl.CostEstimate(flops=flops, bytes_accessed=moved, transcendentals=0),
    )(*[v for v, _ in operands])


def norm_back(weighted, rows_in, scale_vec):
    return scale_vec * weighted - rows_in * scale_vec**3 * jnp.mean(
        weighted * rows_in, axis=-1, keepdims=True
    )


def mix(left, right):
    return jnp.dot(left, right, preferred_element_type=F32)


def mix_back(left, right):
    return lax.dot_general(left, right, (((1,), (1,)), ((), ())), preferred_element_type=F32)


def on_device(
    grid,
    inputs,
    seg_ids,
    norm_in,
    proj_y,
    proj_x,
    conv_weight,
    conv_bias,
    rate_weight,
    rate_bias,
    input_weight,
    input_bias,
    decay_param,
    proj_out,
    norm_mlp,
    mlp_gate,
    mlp_up,
    mlp_down,
    cotangent,
):
    nx, ny, nz, nc = (grid.n[p] for p in "xyzc")
    x, y, z, c = (grid.index(p) for p in "xyzc")
    micro, step, depth = inputs.shape
    chains = micro * ny
    length = nx * step
    shard = proj_x.shape[0]

    gain_in = norm_in.astype(F32)[:, None]
    gain_mlp = norm_mlp.astype(F32)[:, None]

    def gained(matrix, gain):
        return (matrix.astype(F32) * gain).astype(BF16)

    width = proj_x.shape[1] // (nx * ny)
    ff_width = mlp_down.shape[1] // (nx * ny)
    plane = nx * ny * shard
    width = proj_x.shape[1] // (nx * ny)
    ff_width = mlp_down.shape[1] // (nx * ny)
    plane = nx * ny * shard
    slope = -8.0 * jax.nn.softplus(-decay_param)
    slope_back = 8.0 * jax.nn.sigmoid(-decay_param)
    small = jnp.concatenate(
        [conv_weight, conv_bias[None], rate_bias[None], input_bias[None], slope[None]], axis=0
    )
    share = small.shape[1]
    heads, block = rate_weight.shape[0], rate_weight.shape[1]
    per = nz // ny
    packed = pack_small(rate_weight, input_weight, small)
    beside = [grid.shift(seg_ids, "y", r) for r in range(1, ny)]
    weights_in = grid.columns_of(
        [gained(proj_x, gain_in), gained(proj_y, gain_in), proj_out]
    ).reshape(plane, 3 * width)
    mix_all = grid.all_rows(weights_in)
    half = lax.dynamic_index_in_dim(after(packed, weights_in), c, 0, keepdims=False)
    others = lax.optimization_barrier([grid.shift(half, "z", r) for r in range(1, nz)])
    by_z = lax.dynamic_slice_in_dim(grid.place([half, *others], "z"), y * per, per, 0)
    by_x = grid.place([by_z] + [grid.shift(by_z, "x", r) for r in range(1, nx)], "x")
    by_x = jnp.moveaxis(by_x, 0, 1).reshape(per * nx, *half.shape)
    halves = grid.place([by_x] + [grid.shift(by_x, "c", r) for r in range(1, nc)], "c")
    gates, vec = unpack_small(halves, x, per, heads)
    own_rows = grid.turn(after(inputs, *others, *beside))
    source = own_rows.astype(F32)
    normed, in_hop = grid.spread(own_rows, halves, normed=True)
    ahead = grid.rows_ahead(own_rows[:, step - 2 * HALO :])
    ahead = jnp.stack([ahead] + [grid.shift(ahead, "y", r) for r in range(1, ny)], axis=1)
    ahead = ahead.reshape(chains * 2 * HALO, depth)
    pieces = [gained(mlp_gate, gain_mlp), gained(mlp_up, gain_mlp), mlp_down]
    pieces = [after(p, weights_in) for p in pieces]
    weights_ff = grid.columns_of(pieces, *in_hop).reshape(plane, -1)
    ff_in = grid.all_rows(weights_ff[:, : 2 * ff_width])
    ff_down = grid.all_rows(weights_ff[:, 2 * ff_width :])

    segments = jnp.stack([seg_ids, *beside], axis=1)
    padded = jnp.pad(segments, ((0, 0), (0, 0), (HALO, 0)), constant_values=-1)
    near = lax.dynamic_slice_in_dim(padded, z * length, length + HALO, 2)
    here = near[:, :, HALO:]
    same = [jnp.ones_like(here, dtype=F32)]
    for k in range(1, TAPS):
        same.append((near[:, :, HALO - k : HALO - k + length] == here).astype(F32))
    same = jnp.stack(same + [jnp.zeros_like(same[0])] * (8 - TAPS), axis=-1)
    same = same.reshape(chains, length, 8)
    order = ((x - jnp.arange(nx, dtype=jnp.int32)) % nx).astype(jnp.int32)

    mix_all = after(mix_all, vec, same)
    mix_x, mix_y, mix_out = (mix_all[:, i * width : (i + 1) * width] for i in range(3))
    drive = mix(normed, mix_x).astype(BF16).reshape(chains, nx, step, width)
    ahead = ahead.astype(F32)
    ahead = ahead * lax.rsqrt(jnp.mean(ahead * ahead, axis=-1, keepdims=True) + NORM_EPS)
    halo = mix(ahead.astype(BF16), mix_x).astype(BF16).reshape(chains, 2 * HALO, width)
    halo = halo[:, HALO:].astype(F32)
    own_cot = grid.turn(after(cotangent, drive))
    pre_y = mix(normed, mix_y)
    branch_y, gelu_y_back = jax.vjp(jax.nn.gelu, pre_y)
    shape = (chains, length, width)
    turned = (chains, nx, step, width)
    conv, rate, gate_in, state, prods, ends = scan_call(
        forward_kernel,
        chains,
        [(order, False), (drive, True), (halo, True), (same, True), (vec, False), (gates, False)],
        [(shape, F32, True)] * 3 + [(turned, F32, True)] * 2 + [((chains, 8, width), F32, True)],
        [(length + HALO, width), (length, width), (length, width)],
        flops=8 * chains * length * width * width,
    )

    def carry_from(summary, sign):
        carry = jnp.zeros((chains, 1, width), F32)
        for r in reversed(range(1, nz)):
            got = grid.shift(summary, "z", sign * r, wrap=False)
            carry = got[:, 1:2] + got[:, 0:1] * carry
        return carry

    rows_cot, cot_hop = grid.spread(own_cot, ends)
    start = carry_from(ends[:, 0:2], 1)
    hidden = (state + prods * start[:, None]).astype(BF16)
    hidden_f = hidden.reshape(chains * length, width).astype(F32)
    mixed = after((branch_y * hidden_f).astype(BF16), *cot_hop)
    resid = source + grid.collect(mix_back(mixed, mix_out).astype(BF16), micro)

    scale_mlp = lax.rsqrt(jnp.mean(resid * resid, axis=-1, keepdims=True) + NORM_EPS)
    normed_mlp, _ = grid.spread((resid * scale_mlp).astype(BF16))
    pre_ff = mix(normed_mlp, after(ff_in, normed_mlp))
    pre_gate, pre_up = pre_ff[:, :ff_width], pre_ff[:, ff_width:]
    activated, gelu_gate_back = jax.vjp(jax.nn.gelu, pre_gate)
    product = (activated * pre_up).astype(BF16)
    sum_down = WeightSum(grid, rows_cot, product)
    sum_down.lend()
    sum_down.meet()
    ff_down = after(ff_down, sum_down.mine)
    grad_prod = mix(rows_cot, ff_down)
    grad_gate = gelu_gate_back(grad_prod * pre_up)[0].astype(BF16)
    grad_up = (grad_prod * activated).astype(BF16)
    grad_ff = jnp.concatenate([grad_gate, grad_up], axis=1)
    sum_ff = WeightSum(grid, normed_mlp, grad_ff)
    sum_ff.lend()
    part_mlp = mix_back(after(grad_ff, *sum_ff.lent), ff_in).astype(BF16)
    sum_ff.right = after(grad_ff, part_mlp)
    sum_ff.meet()
    sum_ff.mine = jnp.concatenate([sum_ff.mine.astype(BF16), sum_down.mine.astype(BF16)], axis=1)
    sum_ff.along_z()
    weighted_mlp = grid.collect(part_mlp, micro, sum_ff.mine)
    grad_resid = own_cot.astype(F32) + norm_back(weighted_mlp, resid, scale_mlp)
    part_out = mix_back(after(product, weighted_mlp), ff_down).astype(BF16)
    grad_branch, _ = grid.spread(grad_resid.astype(BF16), part_out)
    block_out = resid + grid.collect(after(part_out, grad_branch), micro)

    grad_mixed = mix(grad_branch, mix_out)
    grad_pre_y = gelu_y_back(grad_mixed * hidden_f)[0].astype(BF16)
    grad_state = (grad_mixed * branch_y).astype(BF16).reshape(turned)
    d_local, d_prods, d_ends = scan_call(
        reverse_kernel,
        chains,
        [(order, False), (grad_state, True), (same, True), (vec, False), (rate, True)],
        [(shape, F32, True)] * 2 + [((chains, 8, width), F32, True)],
        [(length, width), (length + HALO, width)],
        flops=40 * chains * length * width,
    )
    d_carry = carry_from(d_ends[:, 0:2], -1)
    d_drive, head, *d_pre, sums = scan_call(
        final_kernel,
        chains,
        [
            (order, False),
            (drive, True),
            (halo, True),
            (same, True),
            (vec, False),
            (gates, False),
            (conv, True),
            (rate, True),
            (gate_in, True),
            (state, True),
            (prods, True),
            (start, True),
            (d_local, True),
            (d_prods, True),
            (d_carry, True),
        ],
        [
            (turned, F32, True),
            ((chains, HALO, width), F32, True),
            (shape, BF16, True),
            (shape, BF16, True),
            ((8, width), F32, False),
        ],
        [(length + HALO, width), (length + 2 * HALO, width)],
        flops=8 * chains * length * width * width,
    )
    behind = grid.shift(head, "z", -1, wrap=False)
    chunk = lax.broadcasted_iota(jnp.int32, (1, nx, 1, 1), 1)
    tail = jnp.pad(behind, ((0, 0), (step - HALO, 0), (0, 0)))[:, None]
    d_drive = d_drive + jnp.where(chunk == (x - (nx - 1)) % nx, tail, 0.0)
    grad_drive = d_drive.astype(BF16).reshape(chains * length, width)
    part_in = (mix_back(grad_pre_y, mix_y) + mix_back(grad_drive, mix_x)).astype(BF16)
    part_in = after(part_in, block_out)
    both = jnp.concatenate([grad_pre_y, grad_drive], axis=1)
    sum_in = WeightSum(grid, normed, after(both, part_in))
    sum_out = WeightSum(grid, grad_branch, after(mixed, part_in))
    sum_in.lend()
    sum_out.lend()
    sum_in.meet()
    sum_out.meet()
    sum_in.mine = jnp.concatenate([sum_in.mine.astype(BF16), sum_out.mine.astype(BF16)], axis=1)
    conv_low = after(conv, part_in).reshape(chains * length, width).astype(BF16)
    gate_dense = [
        lax.dot_general(
            conv_low,
            d.reshape(chains * length, width),
            (((0,), (0,)), ((), ())),
            preferred_element_type=F32,
        )
        for d in d_pre
    ]
    rest = jnp.zeros((8, block), F32)
    blocks = []
    for h in range(per * heads):
        at = slice(h * block, (h + 1) * block)
        blocks.append(jnp.concatenate([gate_dense[0][at, at], sums[:, at], rest], axis=0))
        blocks.append(jnp.concatenate([gate_dense[1][at, at], rest, rest], axis=0))
    blocks = jnp.stack(blocks).astype(BF16).reshape(per, heads, 2, block + 16, block)
    kept = lax.dynamic_index_in_dim(blocks, c, 2, keepdims=False).astype(F32)
    for r in range(1, nc):
        given = lax.dynamic_index_in_dim(blocks, (c + r) % nc, 2, keepdims=False)
        kept = kept + grid.shift(given, "c", r).astype(F32)
    blocks = kept.astype(BF16)
    weighted_in = grid.collect(part_in, micro, sum_in.mine, blocks)
    weighted_in = after(weighted_in, sum_ff.done)
    sum_in.along_z(sum_ff.done)
    grad_gate_w, grad_up_w, grad_down_w = sum_ff.finish(3)
    block_out = grid.turn(block_out.astype(BF16), back=True)
    grad_y_w, grad_x_w, grad_out_w = sum_in.finish(3)
    scale_in = lax.rsqrt(jnp.mean(source * source, axis=-1, keepdims=True) + NORM_EPS)
    grad_source = grad_resid + norm_back(weighted_in, source, scale_in)
    grad_source = grid.turn(grad_source.astype(BF16), back=True)

    def gain_grad(*pairs):
        return sum(jnp.sum(w.astype(F32) * g, axis=1) for w, g in pairs)

    grad_norm_in = gain_grad((proj_y, grad_y_w), (proj_x, grad_x_w))
    grad_norm_mlp = gain_grad((mlp_gate, grad_gate_w), (mlp_up, grad_up_w))

    blocks = grid.total(blocks, "z", grad_gate_w)
    got = [
        [grid.shift_plane(blocks, ry, rx) if ry or rx else blocks for rx in range(nx)]
        for ry in range(ny)
    ]
    by_y = grid.place([grid.place(row, "x") for row in got], "y")
    mine = lax.dynamic_index_in_dim(
        by_y.reshape(ny * nx * per, *blocks.shape[1:]), z * nx + x, 0, keepdims=False
    )
    mats = grid.gather(mine, "c").astype(F32)
    sums_own = jnp.moveaxis(mats[0, :, block : block + 8], 0, 1).reshape(8, share)
    mats = mats[:, :, :block]
    return (
        block_out,
        grad_source,
        grad_norm_in,
        grad_y_w * gain_in,
        grad_x_w * gain_in,
        sums_own[0:4],
        sums_own[4],
        mats[0],
        sums_own[5],
        mats[1],
        sums_own[6],
        sums_own[7] * slope_back,
        grad_out_w,
        grad_norm_mlp,
        grad_gate_w * gain_mlp,
        grad_up_w * gain_mlp,
        grad_down_w,
    )


def solution(mesh):
    grid = Grid(mesh.shape["seq"], mesh.shape["blk"])
    every = ("seq", "blk")
    placed = (
        P(None, every, None),
        P(None, "seq"),
        P(every),
        P(every, None),
        P(every, None),
        P(None, "blk"),
        P("blk"),
        P("blk", None, None),
        P("blk"),
        P("blk", None, None),
        P("blk"),
        P("blk"),
        P(every, None),
        P(every),
        P(every, None),
        P(every, None),
        P(every, None),
        P(None, every, None),
    )
    return jax.shard_map(
        functools.partial(on_device, grid),
        mesh=mesh,
        in_specs=placed,
        out_specs=(
            P(None, every, None),
            P(None, every, None),
            P(every),
            P(every, None),
            P(every, None),
            P(None, "blk"),
            P("blk"),
            P("blk", None, None),
            P("blk"),
            P("blk", None, None),
            P("blk"),
            P("blk"),
            P(every, None),
            P(every),
            P(every, None),
            P(every, None),
            P(every, None),
        ),
        check_vma=False,
    )
```

```python
import functools

import jax
import jax.numpy as jnp
from jax import lax
from jax.experimental import pallas as pl
from jax.experimental.pallas import tpu as pltpu
from jax.sharding import PartitionSpec as P

NORM_EPS = 1e-06
F32 = jnp.float32
BF16 = jnp.bfloat16
TAPS = 4
HALO = 8


class Grid:
    def __init__(self, n_seq, n_blk):
        core = 2 if n_seq % 2 == 0 else 1
        nx = max(d for d in range(1, n_blk + 1) if d * d <= n_blk and n_blk % d == 0)
        self.n = {"y": n_seq // core, "c": core, "z": n_blk // nx, "x": nx}
        self.n_blk = n_blk

    def index(self, part):
        seq, blk = lax.axis_index("seq"), lax.axis_index("blk")
        return {
            "y": seq // self.n["c"],
            "c": seq % self.n["c"],
            "z": blk // self.n["x"],
            "x": blk % self.n["x"],
        }[part]

    def shift(self, value, part, by, wrap=True):
        outer, inner, axis = {
            "y": ("y", "c", "seq"),
            "c": ("y", "c", "seq"),
            "z": ("z", "x", "blk"),
            "x": ("z", "x", "blk"),
        }[part]
        pairs = []
        for o in range(self.n[outer]):
            for i in range(self.n[inner]):
                p = (o if part == outer else i) + by
                if not wrap and not 0 <= p < self.n[part]:
                    continue
                p = p % self.n[part]
                to = (p, i) if part == outer else (o, p)
                pairs.append((o * self.n[inner] + i, to[0] * self.n[inner] + to[1]))
        return lax.ppermute(value, axis, pairs)

    def shift_plane(self, value, by_y, by_x):
        ny, nc, nz, nx = (self.n[p] for p in "yczx")
        pairs = []
        for y in range(ny):
            for c in range(nc):
                for z in range(nz):
                    for x in range(nx):
                        to = (((y + by_y) % ny * nc + c) * nz + z) * nx + (x + by_x) % nx
                        pairs.append((((y * nc + c) * nz + z) * nx + x, to))
        return lax.ppermute(value, ("seq", "blk"), pairs)

    def rows_ahead(self, rows, *late):
        ny, nc, nz, nx = (self.n[p] for p in "yczx")
        out = None
        for x in range(nx):
            pairs = []
            for s in range(ny * nc):
                for z in range(nz - 1):
                    pairs.append(((s * nz + z) * nx + nx - 1, (s * nz + z + 1) * nx + x))
            got = after(lax.ppermute(rows, ("seq", "blk"), pairs), *late)
            out = got if out is None else out + got
        return out

    def place(self, by_shift, part):
        n, me = self.n[part], self.index(part)
        if n == 1:
            return by_shift[0][None]
        if n == 2:
            here, there = by_shift
            low = me == 0
            return jnp.stack([jnp.where(low, here, there), jnp.where(low, there, here)])
        out = jnp.zeros((n, *by_shift[0].shape), by_shift[0].dtype)
        for r, value in enumerate(by_shift):
            out = lax.dynamic_update_index_in_dim(out, value, (me - r) % n, 0)
        return out

    def gather(self, value, part):
        n = self.n[part]
        return self.place([value] + [self.shift(value, part, r) for r in range(1, n)], part)

    def exchange(self, value, part, dim):
        n, me = self.n[part], self.index(part)
        got = []
        for r in range(n):
            piece = lax.dynamic_index_in_dim(value, (me + r) % n, dim, keepdims=False)
            got.append(self.shift(piece, part, r) if r else piece)
        return self.place(got, part)

    def total(self, value, part, *late):
        out = value.astype(F32)
        for r in range(1, self.n[part]):
            out = out + after(self.shift(value, part, r), *late).astype(F32)
        return out.astype(value.dtype)

    def turn(self, value, back=False):
        ny, nc, nz = self.n["y"], self.n["c"], self.n["z"]
        places = [
            (y * nc + c) * nz + z for c in range(nc) for z in range(nz) for y in range(ny)
        ]
        width = value.shape[-1] // len(places)
        if width % 128:
            cut = value.reshape(*value.shape[:-1], *((nc, nz, ny) if back else (ny, nc, nz)), width)
            k = value.ndim - 1
            order = (k + 2, k, k + 1) if back else (k + 1, k + 2, k)
            return cut.transpose(tuple(range(k)) + order + (k + 3,)).reshape(value.shape)

        def kernel(src, dst):
            for k, place in enumerate(places):
                here, there = pl.ds(k * width, width), pl.ds(place * width, width)
                if back:
                    dst[:, :, there] = src[:, :, here]
                else:
                    dst[:, :, here] = src[:, :, there]

        return pl.pallas_call(
            kernel,
            out_shape=jax.ShapeDtypeStruct(value.shape, value.dtype),
            cost_estimate=pl.CostEstimate(flops=0, bytes_accessed=4 * value.size, transcendentals=0),
        )(value)

    def spread(self, shard, *late, normed=False):
        nx, ny = self.n["x"], self.n["y"]
        micro, step, width = shard.shape
        got = {(0, 0): shard}
        for r in range(1, nx):
            got[0, r] = after(self.shift(shard, "x", r), *late)
        for r in range(1, ny):
            got[r, 0] = after(self.shift(shard, "y", r), *late)
        hop = [v for k, v in got.items() if k != (0, 0)]
        out = []
        for m in range(micro):
            for ry in range(ny):
                for rx in range(nx):
                    if ry == 0 or rx == 0:
                        out.append((got[ry, rx], m))
                    elif m % 2 == 0:
                        out.append((self.shift(got[0, rx][m], "y", ry), None))
                    else:
                        out.append((self.shift(got[ry, 0][m], "x", rx), None))
        rows = assemble_rows(out, step, width, normed)
        return rows.reshape(len(out) * step, width), hop

    def collect(self, partial, micro, *late):
        nx, ny = self.n["x"], self.n["y"]
        part = partial.reshape(micro, ny, nx, -1, partial.shape[1])
        out = []
        for m in range(micro):
            if m % 2 == 0:
                held = part[m, 0].astype(F32)
                for r in range(1, ny):
                    held = held + after(self.shift(part[m, r], "y", -r), *late).astype(F32)
                last, n = "x", nx
            else:
                held = part[m, :, 0].astype(F32)
                for r in range(1, nx):
                    held = held + after(self.shift(part[m, :, r], "x", -r), *late).astype(F32)
                last, n = "y", ny
            total = held[0]
            for r in range(1, n):
                total = total + self.shift(held[r].astype(BF16), last, -r).astype(F32)
            out.append(total)
        return jnp.stack(out)

    def columns_of(self, pieces, *late):
        nx, ny = self.n["x"], self.n["y"]
        x, y = self.index("x"), self.index("y")

        def take(yy, xx):
            out = []
            for w in pieces:
                width = w.shape[1] // (nx * ny)
                out.append(lax.dynamic_slice_in_dim(w, (yy * nx + xx) * width, width, 1))
            return out[0] if len(out) == 1 else jnp.concatenate(out, axis=1)

        rows = []
        for ry in range(ny):
            got = []
            for rx in range(nx):
                piece = take((y + ry) % ny, (x + rx) % nx)
                got.append(after(self.shift_plane(piece, ry, rx), *late) if ry or rx else piece)
            rows.append(self.place(got, "x"))
        return self.place(rows, "y")

    def z_groups(self):
        nz, nx = self.n["z"], self.n["x"]
        return [[z * nx + x for z in range(nz)] for x in range(nx)]

    def all_rows(self, block):
        ny, nc, nz, nx = (self.n[p] for p in "yczx")
        groups = [
            [((y * nc + c) * nz + z) * nx + x for c in range(nc) for z in range(nz)]
            for y in range(ny)
            for x in range(nx)
        ]
        return lax.all_gather(
            block, ("seq", "blk"), axis=0, tiled=True, axis_index_groups=groups
        )

    def to_owners(self, done, *late):
        nx, ny = self.n["x"], self.n["y"]
        x, y = self.index("x"), self.index("y")
        rows = []
        for ry in range(ny):
            got = []
            for rx in range(nx):
                piece = lax.dynamic_slice(
                    done, ((y + ry) % ny, (x + rx) % nx, 0, 0), (1, 1, *done.shape[2:])
                )[0, 0]
                got.append(after(self.shift_plane(piece, ry, rx), *late) if ry or rx else piece)
            rows.append(self.place(got, "x"))
        return self.place(rows, "y")


class WeightSum:
    def __init__(self, grid, left, right):
        self.grid, self.left, self.right = grid, left, right
        self.share = left.shape[1] // grid.n["c"]

    def product(self, core):
        cut = lax.dynamic_slice_in_dim(self.left, core * self.share, self.share, 1)
        return lax.dot_general(
            cut, self.right, (((0,), (0,)), ((), ())), preferred_element_type=F32
        )

    def lend(self):
        nc, c = self.grid.n["c"], self.grid.index("c")
        self.lent = [self.product((c + s) % nc).astype(BF16) for s in range(1, nc)]

    def meet(self):
        mine = self.product(self.grid.index("c"))
        for s, lent in enumerate(self.lent):
            mine = mine + self.grid.shift(lent, "c", s + 1).astype(F32)
        self.mine = mine

    def along_z(self, *late):
        self.done = lax.psum_scatter(
            after(self.mine.astype(BF16), *late),
            "blk",
            scatter_dimension=0,
            tiled=True,
            axis_index_groups=self.grid.z_groups(),
        )

    def finish(self, *cuts):
        grid = self.grid
        ny, nx = grid.n["y"], grid.n["x"]
        done = self.done.reshape(ny, nx, -1, self.done.shape[1])
        side = grid.to_owners(done)
        return [
            jnp.concatenate(
                [
                    side[yy, xx, :, at : at + width].astype(F32)
                    for yy in range(ny)
                    for xx in range(nx)
                    for at, width in cut
                ],
                axis=1,
            )
            for cut in cuts
        ]


def after(value, *others):
    return lax.optimization_barrier((value, *others))[0]


def assemble_rows(pieces, step, width, normed):
    arrays = []
    for value, _ in pieces:
        if not any(value is a for a in arrays):
            arrays.append(value)
    which = [next(i for i, a in enumerate(arrays) if a is value) for value, _ in pieces]
    cut = 32 if step % 32 == 0 else step

    def kernel(*refs):
        out = refs[-1]
        for k, (_, lead) in enumerate(pieces):
            ref = refs[which[k]]
            block = ref[...] if lead is None else ref[lead]
            if normed:
                block = block.astype(F32)
                square = jnp.mean(block * block, axis=-1, keepdims=True)
                block = (block * lax.rsqrt(square + NORM_EPS)).astype(out.dtype)
            out[k] = block

    specs = []
    for a in arrays:
        if a.ndim == 2:
            specs.append(pl.BlockSpec((cut, width), lambda i: (i, 0)))
        else:
            specs.append(pl.BlockSpec((a.shape[0], cut, width), lambda i: (0, i, 0)))
    count = len(pieces)
    return pl.pallas_call(
        kernel,
        grid=(step // cut,),
        in_specs=specs,
        out_specs=pl.BlockSpec((count, cut, width), lambda i: (0, i, 0)),
        out_shape=jax.ShapeDtypeStruct((count, step, width), BF16),
        compiler_params=pltpu.CompilerParams(vmem_limit_bytes=32 * 1024 * 1024),
        cost_estimate=pl.CostEstimate(
            flops=0, bytes_accessed=4 * count * step * width, transcendentals=0
        ),
    )(*arrays)


def pack_small(rate_weight, input_weight, small):
    heads, block, _ = rate_weight.shape
    rows = heads * block
    by_head = jnp.moveaxis(small.reshape(8, heads, block), 1, 0)
    by_head = jnp.pad(by_head, ((0, 0), (0, 8), (0, 0))).reshape(heads * 16, block)

    def kernel(rate, gate_in, values, out):
        for h in range(heads):
            out[0, h * block : (h + 1) * block] = rate[h]
            out[1, h * block : (h + 1) * block] = gate_in[h]
        rest = values[...]
        for t in range(3):
            high = rest.astype(BF16)
            at = rows + t * heads * 16
            out[0, at : at + heads * 16] = high
            out[1, at : at + heads * 16] = high
            rest = rest - high.astype(F32)

    return pl.pallas_call(
        kernel,
        out_shape=jax.ShapeDtypeStruct((2, rows + 48 * heads, block), BF16),
        cost_estimate=pl.CostEstimate(flops=0, bytes_accessed=8 * rows * block, transcendentals=0),
    )(rate_weight, input_weight, by_head)


def unpack_small(halves, place, per, heads):
    _, _, depth, block = halves.shape
    rows = heads * block
    width = per * rows

    def kernel(which, share, gates, vec):
        row = lax.broadcasted_iota(jnp.int32, (block, width), 0)
        column = lax.broadcasted_iota(jnp.int32, (block, width), 1)
        total = jnp.zeros((16, width), F32)
        for p in range(per):
            for h in range(heads):
                head = p * heads + h
                pick = jnp.where(column == row + head * block, 1.0, 0.0).astype(BF16)
                for g in range(2):
                    part = share[g, p, h * block : (h + 1) * block]
                    gates[g, head * block : (head + 1) * block] = jnp.dot(
                        part, pick, preferred_element_type=F32
                    ).astype(BF16)
                for t in range(3):
                    at = rows + (t * heads + h) * 16
                    total = total + jnp.dot(
                        share[0, p, at : at + 16], pick, preferred_element_type=F32
                    )
        vec[...] = total[0:8]

    return pl.pallas_call(
        kernel,
        grid_spec=pltpu.PrefetchScalarGridSpec(
            num_scalar_prefetch=1,
            grid=(1,),
            in_specs=[pl.BlockSpec((2, per, depth, block), lambda i, which: (0, which[0], 0, 0))],
            out_specs=[
                pl.BlockSpec((2, width, width), lambda i, which: (0, 0, 0)),
                pl.BlockSpec((8, width), lambda i, which: (0, 0)),
            ],
        ),
        out_shape=[
            jax.ShapeDtypeStruct((2, width, width), BF16),
            jax.ShapeDtypeStruct((8, width), F32),
        ],
        compiler_params=pltpu.CompilerParams(vmem_limit_bytes=32 * 1024 * 1024),
        cost_estimate=pl.CostEstimate(
            flops=0, bytes_accessed=4 * width * width, transcendentals=0
        ),
    )(place.astype(jnp.int32)[None], halves)


def decay_terms(rate, slope):
    log_decay = rate * slope
    small = 1.0 / 40320.0
    for div in (5040.0, 720.0, 120.0, 24.0, 6.0, 2.0, 1.0):
        small = small * log_decay + 1.0 / div
    less = jnp.where(log_decay < -0.4, jnp.exp(log_decay) - 1.0, log_decay * small)
    decay = 1.0 + less
    square = -less * (1.0 + decay)
    return decay, square


def split_dot(value, weight):
    high = value.astype(BF16)
    rest = (value - high.astype(F32)).astype(BF16)
    return jnp.dot(high, weight, preferred_element_type=F32) + jnp.dot(
        rest, weight, preferred_element_type=F32
    )


def forward_kernel(order, u, halo, same, vec, gates, conv, rate, gate_in, state, prods, ends, rows, keep_a, keep_b):
    nx, step = u.shape[1], u.shape[2]
    length = nx * step
    rows[0:HALO] = halo[0]
    for i in range(nx):
        rows[HALO + i * step : HALO + (i + 1) * step] = u[0, order[i]].astype(F32)
    filtered = vec[4:5] + rows[HALO : HALO + length] * vec[0:1]
    for k in range(1, TAPS):
        filtered = filtered + rows[HALO - k : HALO - k + length] * same[0, :, k : k + 1] * vec[k : k + 1]
    conv[0] = filtered
    r_gate = jax.nn.sigmoid(split_dot(filtered, gates[0]) + vec[5:6])
    i_gate = jax.nn.sigmoid(split_dot(filtered, gates[1]) + vec[6:7])
    rate[0] = r_gate
    gate_in[0] = i_gate
    decay, square = decay_terms(r_gate, vec[7:8])
    a = decay * same[0, :, 1:2]
    b = jnp.sqrt(square) * i_gate * filtered
    width = a.shape[1]
    tiles = length // 8
    a = a.reshape(tiles, 8, width)
    b = b.reshape(tiles, 8, width)
    row = lax.broadcasted_iota(jnp.int32, (tiles, 8, width), 1)
    for d in (1, 2, 4):
        a_back = jnp.where(row >= d, pltpu.roll(a, d, 1), 1.0)
        b_back = jnp.where(row >= d, pltpu.roll(b, d, 1), 0.0)
        b = b + a * b_back
        a = a * a_back
    keep_a[...] = a.reshape(length, width)
    keep_b[...] = b.reshape(length, width)
    carry_s = jnp.zeros((1, width), F32)
    carry_a = jnp.ones((1, width), F32)
    for t in range(tiles):
        at = keep_a[t * 8 : t * 8 + 8]
        bt = keep_b[t * 8 : t * 8 + 8]
        s = bt + at * carry_s
        p = at * carry_a
        at_row = (t * 8) % step
        state[0, order[t * 8 // step], at_row : at_row + 8] = s
        prods[0, order[t * 8 // step], at_row : at_row + 8] = p
        carry_s = s[7:8]
        carry_a = p[7:8]
    ends[0, 0:1] = carry_a
    ends[0, 1:2] = carry_s
    ends[0, 2:8] = jnp.zeros((6, width), F32)


def reverse_kernel(order, d_state, same, vec, rate, grads, prods, ends, keep_g, keep_a):
    nx, step = d_state.shape[1], d_state.shape[2]
    length = nx * step
    width = rate.shape[2]
    decay, _ = decay_terms(rate[0], vec[7:8])
    a = decay * same[0, :, 1:2]
    keep_a[0:length] = a
    keep_a[length : length + 8] = jnp.ones((8, width), F32)
    for i in range(nx):
        keep_g[i * step : (i + 1) * step] = d_state[0, order[i]].astype(F32)
    first = a[0:1]
    tiles = length // 8
    nxt = keep_a[1 : length + 1].reshape(tiles, 8, width)
    g = keep_g[...].reshape(tiles, 8, width)
    row = lax.broadcasted_iota(jnp.int32, (tiles, 8, width), 1)
    p = nxt
    for d in (1, 2, 4):
        g_ahead = jnp.where(row < 8 - d, pltpu.roll(g, 8 - d, 1), 0.0)
        p_ahead = jnp.where(row < 8 - d, pltpu.roll(p, 8 - d, 1), 1.0)
        g = g + p * g_ahead
        p = p * p_ahead
    keep_g[...] = g.reshape(length, width)
    keep_a[0:length] = p.reshape(length, width)
    carry_g = jnp.zeros((1, width), F32)
    carry_p = jnp.ones((1, width), F32)
    for t in reversed(range(tiles)):
        pt = keep_a[t * 8 : t * 8 + 8]
        gt = keep_g[t * 8 : t * 8 + 8] + pt * carry_g
        pt = pt * carry_p
        grads[0, t * 8 : t * 8 + 8] = gt
        prods[0, t * 8 : t * 8 + 8] = pt
        carry_g = gt[0:1]
        carry_p = pt[0:1]
    ends[0, 0:1] = first * carry_p
    ends[0, 1:2] = first * carry_g
    ends[0, 2:8] = jnp.zeros((6, width), F32)


def final_kernel(
    order, u, halo, same, vec, gates, conv, rate, gate_in, state, prods, start, grads, back, carry,
    d_u, head, d_rate, d_input, sums, rows, tail,
):
    nx, step = u.shape[1], u.shape[2]
    length = nx * step
    width = conv.shape[2]
    d_s = grads[0] + back[0] * carry[0, 0:1]
    for i in range(nx):
        rows[HALO + i * step : HALO + (i + 1) * step] = (
            state[0, order[i]] + prods[0, order[i]] * start[0, 0:1]
        )
    rows[HALO - 1 : HALO] = start[0, 0:1]
    s_prev = rows[HALO - 1 : HALO - 1 + length]
    r_gate, i_gate, filtered = rate[0], gate_in[0], conv[0]
    decay, square = decay_terms(r_gate, vec[7:8])
    inverse = lax.rsqrt(jnp.maximum(square, 1e-37))
    scale = square * inverse
    a = decay * same[0, :, 1:2]
    d_scaled = d_s * i_gate * filtered
    d_log = d_s * s_prev * a - d_scaled * (decay * decay) * inverse
    d_i = d_s * scale * filtered * i_gate * (1.0 - i_gate)
    d_r = d_log * vec[7:8] * r_gate * (1.0 - r_gate)
    d_r_low = d_r.astype(BF16)
    d_i_low = d_i.astype(BF16)
    d_rate[0] = d_r_low
    d_input[0] = d_i_low
    back_dims = (((1,), (1,)), ((), ()))
    d_c = (
        d_s * scale * i_gate
        + lax.dot_general(d_r_low, gates[0], back_dims, preferred_element_type=F32)
        + lax.dot_general(d_i_low, gates[1], back_dims, preferred_element_type=F32)
    )
    rows[0:HALO] = halo[0]
    for i in range(nx):
        rows[HALO + i * step : HALO + (i + 1) * step] = u[0, order[i]].astype(F32)

    def column(value):
        return jnp.sum(value, axis=0, keepdims=True)

    parts = [column(d_c * rows[HALO : HALO + length])]
    tail[0:HALO] = jnp.zeros((HALO, width), F32)
    tail[HALO + length : 2 * HALO + length] = jnp.zeros((HALO, width), F32)
    d_rows = d_c * vec[0:1]
    d_head = jnp.zeros((HALO, width), F32)
    for k in range(1, TAPS):
        masked = d_c * same[0, :, k : k + 1]
        parts.append(column(masked * rows[HALO - k : HALO - k + length]))
        tail[HALO : HALO + length] = masked * vec[k : k + 1]
        d_rows = d_rows + tail[HALO + k : HALO + k + length]
        d_head = d_head + tail[k : k + HALO]
    for i in range(nx):
        d_u[0, order[i]] = d_rows[i * step : (i + 1) * step]
    head[0] = d_head
    parts += [column(d_c), column(d_r), column(d_i), column(d_log * r_gate)]

    @pl.when(pl.program_id(0) == 0)
    def _():
        sums[...] = jnp.zeros_like(sums)

    for i, value in enumerate(parts):
        sums[i : i + 1] += value


def chain_spec(*dims):
    return pl.BlockSpec((1, *dims), lambda i: (i,) + (0,) * len(dims))


def whole_spec(*dims):
    return pl.BlockSpec(dims, lambda i: (0,) * len(dims))


def scan_call(kernel, chains, operands, outs, scratch, flops):
    specs = [pl.BlockSpec(memory_space=pltpu.SMEM)]
    for value, chained in operands[1:]:
        specs.append(chain_spec(*value.shape[1:]) if chained else whole_spec(*value.shape))
    shapes, out_specs = [], []
    for shape, dtype, chained in outs:
        shapes.append(jax.ShapeDtypeStruct(shape, dtype))
        out_specs.append(chain_spec(*shape[1:]) if chained else whole_spec(*shape))
    moved = sum(v.size * v.dtype.itemsize for v, _ in operands)
    moved += sum(s.size * s.dtype.itemsize for s in shapes)
    return pl.pallas_call(
        kernel,
        grid=(chains,),
        in_specs=specs,
        out_specs=out_specs,
        out_shape=shapes,
        scratch_shapes=[pltpu.VMEM(s, F32) for s in scratch],
        compiler_params=pltpu.CompilerParams(vmem_limit_bytes=48 * 1024 * 1024),
        cost_estimate=pl.CostEstimate(flops=flops, bytes_accessed=moved, transcendentals=0),
    )(*[v for v, _ in operands])


def norm_back(weighted, rows_in, scale_vec):
    return scale_vec * weighted - rows_in * scale_vec**3 * jnp.mean(
        weighted * rows_in, axis=-1, keepdims=True
    )


def mix(left, right):
    return jnp.dot(left, right, preferred_element_type=F32)


def mix_back(left, right):
    return lax.dot_general(left, right, (((1,), (1,)), ((), ())), preferred_element_type=F32)


def on_device(
    grid,
    inputs,
    seg_ids,
    norm_in,
    proj_y,
    proj_x,
    conv_weight,
    conv_bias,
    rate_weight,
    rate_bias,
    input_weight,
    input_bias,
    decay_param,
    proj_out,
    norm_mlp,
    mlp_gate,
    mlp_up,
    mlp_down,
    cotangent,
):
    nx, ny, nz, nc = (grid.n[p] for p in "xyzc")
    x, y, z, c = (grid.index(p) for p in "xyzc")
    micro, step, depth = inputs.shape
    chains = micro * ny
    length = nx * step
    shard = proj_x.shape[0]

    gain_in = norm_in.astype(F32)[:, None]
    gain_mlp = norm_mlp.astype(F32)[:, None]

    def gained(matrix, gain):
        return (matrix.astype(F32) * gain).astype(BF16)

    width = proj_x.shape[1] // (nx * ny)
    ff_width = mlp_down.shape[1] // (nx * ny)
    plane = nx * ny * shard
    width = proj_x.shape[1] // (nx * ny)
    ff_width = mlp_down.shape[1] // (nx * ny)
    plane = nx * ny * shard
    slope = -8.0 * jax.nn.softplus(-decay_param)
    slope_back = 8.0 * jax.nn.sigmoid(-decay_param)
    small = jnp.concatenate(
        [conv_weight, conv_bias[None], rate_bias[None], input_bias[None], slope[None]], axis=0
    )
    share = small.shape[1]
    heads, block = rate_weight.shape[0], rate_weight.shape[1]
    per = nz // ny
    packed = pack_small(rate_weight, input_weight, small)
    beside = [grid.shift(seg_ids, "y", r) for r in range(1, ny)]
    weights_in = grid.columns_of(
        [gained(proj_x, gain_in), gained(proj_y, gain_in), proj_out]
    ).reshape(plane, 3 * width)
    mix_all = grid.all_rows(weights_in)
    half = lax.dynamic_index_in_dim(after(packed, weights_in), c, 0, keepdims=False)
    others = lax.optimization_barrier([grid.shift(half, "z", r) for r in range(1, nz)])
    own_rows = grid.turn(after(inputs, weights_in, *beside))
    source = own_rows.astype(F32)
    normed, in_hop = grid.spread(own_rows, *others, normed=True)
    by_z = jnp.stack([half, *others])
    by_z = jnp.stack(
        [
            lax.dynamic_index_in_dim(by_z, (z - y * per - i) % nz, 0, keepdims=False)
            for i in range(per)
        ]
    )
    by_z = after(by_z, *in_hop)
    by_x = grid.place([by_z] + [grid.shift(by_z, "x", r) for r in range(1, nx)], "x")
    by_x = jnp.moveaxis(by_x, 0, 1).reshape(per * nx, *half.shape)
    halves = grid.place([by_x] + [grid.shift(by_x, "c", r) for r in range(1, nc)], "c")
    gates, vec = unpack_small(halves, x, per, heads)
    ahead = grid.rows_ahead(own_rows[:, step - HALO :], vec)
    ahead = jnp.stack([ahead] + [grid.shift(ahead, "y", r) for r in range(1, ny)], axis=1)
    ahead = ahead.reshape(chains * HALO, depth)
    pieces = [gained(mlp_gate, gain_mlp), gained(mlp_up, gain_mlp), mlp_down]
    pieces = [after(p, weights_in) for p in pieces]
    weights_ff = grid.columns_of(pieces, *in_hop).reshape(plane, -1)
    wide = ff_width - ff_width // 3
    ff_cuts = [
        grid.all_rows(
            jnp.concatenate(
                [weights_ff[:, i * ff_width + lo : i * ff_width + hi] for i in range(3)], axis=1
            )
        )
        for lo, hi in ((0, wide), (wide, ff_width))
    ]

    segments = jnp.stack([seg_ids, *beside], axis=1)
    padded = jnp.pad(segments, ((0, 0), (0, 0), (HALO, 0)), constant_values=-1)
    near = lax.dynamic_slice_in_dim(padded, z * length, length + HALO, 2)
    here = near[:, :, HALO:]
    same = [jnp.ones_like(here, dtype=F32)]
    for k in range(1, TAPS):
        same.append((near[:, :, HALO - k : HALO - k + length] == here).astype(F32))
    same = jnp.stack(same + [jnp.zeros_like(same[0])] * (8 - TAPS), axis=-1)
    same = same.reshape(chains, length, 8)
    order = ((x - jnp.arange(nx, dtype=jnp.int32)) % nx).astype(jnp.int32)

    mix_all = after(mix_all, vec, same)
    mix_x, mix_y, mix_out = (mix_all[:, i * width : (i + 1) * width] for i in range(3))
    drive = mix(normed, mix_x).astype(BF16).reshape(chains, nx, step, width)
    ahead = ahead.astype(F32)
    ahead = ahead * lax.rsqrt(jnp.mean(ahead * ahead, axis=-1, keepdims=True) + NORM_EPS)
    halo = mix(ahead.astype(BF16), mix_x).astype(BF16).reshape(chains, HALO, width).astype(F32)
    own_cot = grid.turn(after(cotangent, drive))
    pre_y = mix(normed, mix_y)
    branch_y, gelu_y_back = jax.vjp(jax.nn.gelu, pre_y)
    shape = (chains, length, width)
    turned = (chains, nx, step, width)
    conv, rate, gate_in, state, prods, ends = scan_call(
        forward_kernel,
        chains,
        [(order, False), (drive, True), (halo, True), (same, True), (vec, False), (gates, False)],
        [(shape, F32, True)] * 3 + [(turned, F32, True)] * 2 + [((chains, 8, width), F32, True)],
        [(length + HALO, width), (length, width), (length, width)],
        flops=8 * chains * length * width * width,
    )

    def carry_from(summary, sign):
        carry = jnp.zeros((chains, 1, width), F32)
        for r in reversed(range(1, nz)):
            got = grid.shift(summary, "z", sign * r, wrap=False)
            carry = got[:, 1:2] + got[:, 0:1] * carry
        return carry

    rows_cot, cot_hop = grid.spread(own_cot, ends)
    start = carry_from(ends[:, 0:2], 1)
    hidden = (state + prods * start[:, None]).astype(BF16)
    hidden_f = hidden.reshape(chains * length, width).astype(F32)
    mixed = after((branch_y * hidden_f).astype(BF16), *cot_hop)
    resid = source + grid.collect(mix_back(mixed, mix_out).astype(BF16), micro)

    scale_mlp = lax.rsqrt(jnp.mean(resid * resid, axis=-1, keepdims=True) + NORM_EPS)
    normed_mlp, _ = grid.spread((resid * scale_mlp).astype(BF16))
    part_mlp, mines, outward, last = 0.0, [], [], ()
    for ff in ff_cuts:
        cut = ff.shape[1] // 3
        ff = after(ff, normed_mlp, *last)
        ff_in, ff_down = ff[:, : 2 * cut], ff[:, 2 * cut :]
        pre_ff = mix(normed_mlp, ff_in).astype(BF16)
        pre_gate, pre_up = pre_ff[:, :cut].astype(F32), pre_ff[:, cut:].astype(F32)
        activated, gelu_gate_back = jax.vjp(jax.nn.gelu, pre_gate)
        product = (activated * pre_up).astype(BF16)
        sum_down = WeightSum(grid, rows_cot, product)
        sum_down.lend()
        grad_prod = mix(rows_cot, after(ff_down, *sum_down.lent))
        grad_gate = gelu_gate_back(grad_prod * pre_up)[0].astype(BF16)
        grad_up = (grad_prod * activated).astype(BF16)
        grad_ff = jnp.concatenate([grad_gate, grad_up], axis=1)
        sum_ff = WeightSum(grid, normed_mlp, grad_ff)
        sum_ff.lend()
        sum_down.right = after(product, *sum_ff.lent)
        sum_down.meet()
        part_mlp = part_mlp + mix_back(after(grad_ff, sum_down.mine), ff_in)
        sum_ff.right = after(grad_ff, part_mlp)
        sum_ff.meet()
        mines += [sum_ff.mine.astype(BF16), sum_down.mine.astype(BF16)]
        outward.append((product, ff_down))
        last = (part_mlp, sum_ff.mine)
    part_mlp = part_mlp.astype(BF16)
    sum_ff.mine = jnp.concatenate(mines, axis=1)
    sum_ff.along_z()
    weighted_mlp = grid.collect(part_mlp, micro, sum_ff.mine)
    grad_resid = own_cot.astype(F32) + norm_back(weighted_mlp, resid, scale_mlp)
    part_out = sum(mix_back(after(left, weighted_mlp), right) for left, right in outward)
    part_out = part_out.astype(BF16)
    grad_branch, _ = grid.spread(grad_resid.astype(BF16), part_out)
    block_out = resid + grid.collect(after(part_out, grad_branch), micro)

    grad_mixed = mix(grad_branch, mix_out)
    grad_pre_y = gelu_y_back(grad_mixed * hidden_f)[0].astype(BF16)
    grad_state = (grad_mixed * branch_y).astype(BF16).reshape(turned)
    d_local, d_prods, d_ends = scan_call(
        reverse_kernel,
        chains,
        [(order, False), (grad_state, True), (same, True), (vec, False), (rate, True)],
        [(shape, F32, True)] * 2 + [((chains, 8, width), F32, True)],
        [(length, width), (length + HALO, width)],
        flops=40 * chains * length * width,
    )
    d_carry = carry_from(d_ends[:, 0:2], -1)
    d_drive, head, *d_pre, sums = scan_call(
        final_kernel,
        chains,
        [
            (order, False),
            (drive, True),
            (halo, True),
            (same, True),
            (vec, False),
            (gates, False),
            (conv, True),
            (rate, True),
            (gate_in, True),
            (state, True),
            (prods, True),
            (start, True),
            (d_local, True),
            (d_prods, True),
            (d_carry, True),
        ],
        [
            (turned, F32, True),
            ((chains, HALO, width), F32, True),
            (shape, BF16, True),
            (shape, BF16, True),
            ((8, width), F32, False),
        ],
        [(length + HALO, width), (length + 2 * HALO, width)],
        flops=8 * chains * length * width * width,
    )
    behind = grid.shift(head, "z", -1, wrap=False)
    chunk = lax.broadcasted_iota(jnp.int32, (1, nx, 1, 1), 1)
    tail = jnp.pad(behind, ((0, 0), (step - HALO, 0), (0, 0)))[:, None]
    d_drive = d_drive + jnp.where(chunk == (x - (nx - 1)) % nx, tail, 0.0)
    grad_drive = d_drive.astype(BF16).reshape(chains * length, width)
    part_in = (mix_back(grad_pre_y, mix_y) + mix_back(grad_drive, mix_x)).astype(BF16)
    part_in = after(part_in, block_out)
    both = jnp.concatenate([grad_pre_y, grad_drive], axis=1)
    sum_in = WeightSum(grid, normed, after(both, part_in))
    sum_out = WeightSum(grid, grad_branch, after(mixed, part_in))
    sum_in.lend()
    sum_out.lend()
    sum_in.meet()
    sum_out.meet()
    sum_in.mine = jnp.concatenate([sum_in.mine.astype(BF16), sum_out.mine.astype(BF16)], axis=1)
    conv_low = after(conv, part_in).reshape(chains * length, width).astype(BF16)
    gate_dense = [
        lax.dot_general(
            conv_low,
            d.reshape(chains * length, width),
            (((0,), (0,)), ((), ())),
            preferred_element_type=F32,
        )
        for d in d_pre
    ]
    rest = jnp.zeros((8, block), F32)
    blocks = []
    for h in range(per * heads):
        at = slice(h * block, (h + 1) * block)
        blocks.append(jnp.concatenate([gate_dense[0][at, at], sums[:, at], rest], axis=0))
        blocks.append(jnp.concatenate([gate_dense[1][at, at], rest, rest], axis=0))
    blocks = jnp.stack(blocks).astype(BF16).reshape(per, heads, 2, block + 16, block)
    kept = lax.dynamic_index_in_dim(blocks, c, 2, keepdims=False).astype(F32)
    for r in range(1, nc):
        given = lax.dynamic_index_in_dim(blocks, (c + r) % nc, 2, keepdims=False)
        kept = kept + grid.shift(given, "c", r).astype(F32)
    blocks = kept.astype(BF16)
    weighted_in = grid.collect(part_in, micro, sum_in.mine, blocks)
    weighted_in = after(weighted_in, sum_ff.done)
    sum_in.along_z(sum_ff.done)
    grad_gate_w, grad_up_w, grad_down_w = sum_ff.finish(
        *(
            [(i * wide, wide), (3 * wide + i * (ff_width - wide), ff_width - wide)]
            for i in range(3)
        )
    )
    block_out = grid.turn(block_out.astype(BF16), back=True)
    grad_y_w, grad_x_w, grad_out_w = sum_in.finish(*([(i * width, width)] for i in range(3)))
    scale_in = lax.rsqrt(jnp.mean(source * source, axis=-1, keepdims=True) + NORM_EPS)
    grad_source = grad_resid + norm_back(weighted_in, source, scale_in)
    grad_source = grid.turn(grad_source.astype(BF16), back=True)

    def gain_grad(*pairs):
        return sum(jnp.sum(w.astype(F32) * g, axis=1) for w, g in pairs)

    grad_norm_in = gain_grad((proj_y, grad_y_w), (proj_x, grad_x_w))
    grad_norm_mlp = gain_grad((mlp_gate, grad_gate_w), (mlp_up, grad_up_w))

    blocks = grid.total(blocks, "z", grad_gate_w)
    got = [
        [grid.shift_plane(blocks, ry, rx) if ry or rx else blocks for rx in range(nx)]
        for ry in range(ny)
    ]
    by_y = grid.place([grid.place(row, "x") for row in got], "y")
    mine = lax.dynamic_index_in_dim(
        by_y.reshape(ny * nx * per, *blocks.shape[1:]), z * nx + x, 0, keepdims=False
    )
    mats = grid.gather(mine, "c").astype(F32)
    sums_own = jnp.moveaxis(mats[0, :, block : block + 8], 0, 1).reshape(8, share)
    mats = mats[:, :, :block]
    return (
        block_out,
        grad_source,
        grad_norm_in,
        grad_y_w * gain_in,
        grad_x_w * gain_in,
        sums_own[0:4],
        sums_own[4],
        mats[0],
        sums_own[5],
        mats[1],
        sums_own[6],
        sums_own[7] * slope_back,
        grad_out_w,
        grad_norm_mlp,
        grad_gate_w * gain_mlp,
        grad_up_w * gain_mlp,
        grad_down_w,
    )


def solution(mesh):
    grid = Grid(mesh.shape["seq"], mesh.shape["blk"])
    every = ("seq", "blk")
    placed = (
        P(None, every, None),
        P(None, "seq"),
        P(every),
        P(every, None),
        P(every, None),
        P(None, "blk"),
        P("blk"),
        P("blk", None, None),
        P("blk"),
        P("blk", None, None),
        P("blk"),
        P("blk"),
        P(every, None),
        P(every),
        P(every, None),
        P(every, None),
        P(every, None),
        P(None, every, None),
    )
    return jax.shard_map(
        functools.partial(on_device, grid),
        mesh=mesh,
        in_specs=placed,
        out_specs=(
            P(None, every, None),
            P(None, every, None),
            P(every),
            P(every, None),
            P(every, None),
            P(None, "blk"),
            P("blk"),
            P("blk", None, None),
            P("blk"),
            P("blk", None, None),
            P("blk"),
            P("blk"),
            P(every, None),
            P(every),
            P(every, None),
            P(every, None),
            P(every, None),
        ),
        check_vma=False,
    )
```

```python
import functools

import jax
import jax.numpy as jnp
from jax import lax
from jax.experimental import pallas as pl
from jax.experimental.pallas import tpu as pltpu
from jax.sharding import PartitionSpec as P

NORM_EPS = 1e-06
F32 = jnp.float32
BF16 = jnp.bfloat16
TAPS = 4
HALO = 8


class Grid:
    def __init__(self, n_seq, n_blk):
        core = 2 if n_seq % 2 == 0 else 1
        nx = max(d for d in range(1, n_blk + 1) if d * d <= n_blk and n_blk % d == 0)
        self.n = {"y": n_seq // core, "c": core, "z": n_blk // nx, "x": nx}
        self.n_blk = n_blk

    def index(self, part):
        seq, blk = lax.axis_index("seq"), lax.axis_index("blk")
        return {
            "y": seq // self.n["c"],
            "c": seq % self.n["c"],
            "z": blk // self.n["x"],
            "x": blk % self.n["x"],
        }[part]

    def shift(self, value, part, by, wrap=True):
        outer, inner, axis = {
            "y": ("y", "c", "seq"),
            "c": ("y", "c", "seq"),
            "z": ("z", "x", "blk"),
            "x": ("z", "x", "blk"),
        }[part]
        pairs = []
        for o in range(self.n[outer]):
            for i in range(self.n[inner]):
                p = (o if part == outer else i) + by
                if not wrap and not 0 <= p < self.n[part]:
                    continue
                p = p % self.n[part]
                to = (p, i) if part == outer else (o, p)
                pairs.append((o * self.n[inner] + i, to[0] * self.n[inner] + to[1]))
        return lax.ppermute(value, axis, pairs)

    def shift_plane(self, value, by_y, by_x):
        ny, nc, nz, nx = (self.n[p] for p in "yczx")
        pairs = []
        for y in range(ny):
            for c in range(nc):
                for z in range(nz):
                    for x in range(nx):
                        to = (((y + by_y) % ny * nc + c) * nz + z) * nx + (x + by_x) % nx
                        pairs.append((((y * nc + c) * nz + z) * nx + x, to))
        return lax.ppermute(value, ("seq", "blk"), pairs)

    def rows_ahead(self, rows, *late):
        ny, nc, nz, nx = (self.n[p] for p in "yczx")
        out = None
        for x in range(nx):
            pairs = []
            for s in range(ny * nc):
                for z in range(nz - 1):
                    pairs.append(((s * nz + z) * nx + nx - 1, (s * nz + z + 1) * nx + x))
            got = after(lax.ppermute(rows, ("seq", "blk"), pairs), *late)
            out = got if out is None else out + got
        return out

    def place(self, by_shift, part):
        n, me = self.n[part], self.index(part)
        if n == 1:
            return by_shift[0][None]
        if n == 2:
            here, there = by_shift
            low = me == 0
            return jnp.stack([jnp.where(low, here, there), jnp.where(low, there, here)])
        out = jnp.zeros((n, *by_shift[0].shape), by_shift[0].dtype)
        for r, value in enumerate(by_shift):
            out = lax.dynamic_update_index_in_dim(out, value, (me - r) % n, 0)
        return out

    def gather(self, value, part):
        n = self.n[part]
        return self.place([value] + [self.shift(value, part, r) for r in range(1, n)], part)

    def exchange(self, value, part, dim):
        n, me = self.n[part], self.index(part)
        got = []
        for r in range(n):
            piece = lax.dynamic_index_in_dim(value, (me + r) % n, dim, keepdims=False)
            got.append(self.shift(piece, part, r) if r else piece)
        return self.place(got, part)

    def total(self, value, part, *late):
        out = value.astype(F32)
        for r in range(1, self.n[part]):
            out = out + after(self.shift(value, part, r), *late).astype(F32)
        return out.astype(value.dtype)

    def turn(self, value, back=False):
        ny, nc, nz = self.n["y"], self.n["c"], self.n["z"]
        places = [
            (y * nc + c) * nz + z for c in range(nc) for z in range(nz) for y in range(ny)
        ]
        width = value.shape[-1] // len(places)
        if width % 128:
            cut = value.reshape(*value.shape[:-1], *((nc, nz, ny) if back else (ny, nc, nz)), width)
            k = value.ndim - 1
            order = (k + 2, k, k + 1) if back else (k + 1, k + 2, k)
            return cut.transpose(tuple(range(k)) + order + (k + 3,)).reshape(value.shape)

        def kernel(src, dst):
            for k, place in enumerate(places):
                here, there = pl.ds(k * width, width), pl.ds(place * width, width)
                if back:
                    dst[:, :, there] = src[:, :, here]
                else:
                    dst[:, :, here] = src[:, :, there]

        return pl.pallas_call(
            kernel,
            out_shape=jax.ShapeDtypeStruct(value.shape, value.dtype),
            cost_estimate=pl.CostEstimate(flops=0, bytes_accessed=4 * value.size, transcendentals=0),
        )(value)

    def spread(self, shard, *late, normed=False):
        nx, ny = self.n["x"], self.n["y"]
        micro, step, width = shard.shape
        got = {(0, 0): shard}
        for r in range(1, nx):
            got[0, r] = after(self.shift(shard, "x", r), *late)
        for r in range(1, ny):
            got[r, 0] = after(self.shift(shard, "y", r), *late)
        hop = [v for k, v in got.items() if k != (0, 0)]
        out = []
        for m in range(micro):
            for ry in range(ny):
                for rx in range(nx):
                    if ry == 0 or rx == 0:
                        out.append((got[ry, rx], m))
                    elif m % 2 == 0:
                        out.append((self.shift(got[0, rx][m], "y", ry), None))
                    else:
                        out.append((self.shift(got[ry, 0][m], "x", rx), None))
        rows = assemble_rows(out, step, width, normed)
        return rows.reshape(len(out) * step, width), hop

    def collect(self, partial, micro, *late):
        nx, ny = self.n["x"], self.n["y"]
        part = partial.reshape(micro, ny, nx, -1, partial.shape[1])
        out = []
        for m in range(micro):
            if m % 2 == 0:
                held = part[m, 0].astype(F32)
                for r in range(1, ny):
                    held = held + after(self.shift(part[m, r], "y", -r), *late).astype(F32)
                last, n = "x", nx
            else:
                held = part[m, :, 0].astype(F32)
                for r in range(1, nx):
                    held = held + after(self.shift(part[m, :, r], "x", -r), *late).astype(F32)
                last, n = "y", ny
            total = held[0]
            for r in range(1, n):
                total = total + self.shift(held[r].astype(BF16), last, -r).astype(F32)
            out.append(total)
        return jnp.stack(out)

    def columns_of(self, pieces, *late):
        nx, ny = self.n["x"], self.n["y"]
        x, y = self.index("x"), self.index("y")

        def take(yy, xx):
            out = []
            for w in pieces:
                width = w.shape[1] // (nx * ny)
                out.append(lax.dynamic_slice_in_dim(w, (yy * nx + xx) * width, width, 1))
            return out[0] if len(out) == 1 else jnp.concatenate(out, axis=1)

        rows = []
        for ry in range(ny):
            got = []
            for rx in range(nx):
                piece = take((y + ry) % ny, (x + rx) % nx)
                got.append(after(self.shift_plane(piece, ry, rx), *late) if ry or rx else piece)
            rows.append(self.place(got, "x"))
        return self.place(rows, "y")

    def z_groups(self):
        nz, nx = self.n["z"], self.n["x"]
        return [[z * nx + x for z in range(nz)] for x in range(nx)]

    def all_rows(self, block):
        ny, nc, nz, nx = (self.n[p] for p in "yczx")
        groups = [
            [((y * nc + c) * nz + z) * nx + x for c in range(nc) for z in range(nz)]
            for y in range(ny)
            for x in range(nx)
        ]
        return lax.all_gather(
            block, ("seq", "blk"), axis=0, tiled=True, axis_index_groups=groups
        )

    def to_owners(self, done, *late):
        nx, ny = self.n["x"], self.n["y"]
        x, y = self.index("x"), self.index("y")
        rows = []
        for ry in range(ny):
            got = []
            for rx in range(nx):
                piece = lax.dynamic_slice(
                    done, ((y + ry) % ny, (x + rx) % nx, 0, 0), (1, 1, *done.shape[2:])
                )[0, 0]
                got.append(after(self.shift_plane(piece, ry, rx), *late) if ry or rx else piece)
            rows.append(self.place(got, "x"))
        return self.place(rows, "y")


class WeightSum:
    def __init__(self, grid, left, right):
        self.grid, self.left, self.right = grid, left, right
        self.share = left.shape[1] // grid.n["c"]

    def product(self, core):
        cut = lax.dynamic_slice_in_dim(self.left, core * self.share, self.share, 1)
        return lax.dot_general(
            cut, self.right, (((0,), (0,)), ((), ())), preferred_element_type=F32
        )

    def lend(self):
        nc, c = self.grid.n["c"], self.grid.index("c")
        self.lent = [self.product((c + s) % nc).astype(BF16) for s in range(1, nc)]

    def meet(self):
        mine = self.product(self.grid.index("c"))
        for s, lent in enumerate(self.lent):
            mine = mine + self.grid.shift(lent, "c", s + 1).astype(F32)
        self.mine = mine

    def along_z(self, *late):
        self.done = lax.psum_scatter(
            after(self.mine.astype(BF16), *late),
            "blk",
            scatter_dimension=0,
            tiled=True,
            axis_index_groups=self.grid.z_groups(),
        )

    def finish(self, *cuts):
        grid = self.grid
        ny, nx = grid.n["y"], grid.n["x"]
        done = self.done.reshape(ny, nx, -1, self.done.shape[1])
        side = grid.to_owners(done)
        return [
            jnp.concatenate(
                [
                    side[yy, xx, :, at : at + width].astype(F32)
                    for yy in range(ny)
                    for xx in range(nx)
                    for at, width in cut
                ],
                axis=1,
            )
            for cut in cuts
        ]


def after(value, *others):
    return lax.optimization_barrier((value, *others))[0]


def assemble_rows(pieces, step, width, normed):
    arrays = []
    for value, _ in pieces:
        if not any(value is a for a in arrays):
            arrays.append(value)
    which = [next(i for i, a in enumerate(arrays) if a is value) for value, _ in pieces]
    cut = 32 if step % 32 == 0 else step

    def kernel(*refs):
        out = refs[-1]
        for k, (_, lead) in enumerate(pieces):
            ref = refs[which[k]]
            block = ref[...] if lead is None else ref[lead]
            if normed:
                block = block.astype(F32)
                square = jnp.mean(block * block, axis=-1, keepdims=True)
                block = (block * lax.rsqrt(square + NORM_EPS)).astype(out.dtype)
            out[k] = block

    specs = []
    for a in arrays:
        if a.ndim == 2:
            specs.append(pl.BlockSpec((cut, width), lambda i: (i, 0)))
        else:
            specs.append(pl.BlockSpec((a.shape[0], cut, width), lambda i: (0, i, 0)))
    count = len(pieces)
    return pl.pallas_call(
        kernel,
        grid=(step // cut,),
        in_specs=specs,
        out_specs=pl.BlockSpec((count, cut, width), lambda i: (0, i, 0)),
        out_shape=jax.ShapeDtypeStruct((count, step, width), BF16),
        compiler_params=pltpu.CompilerParams(vmem_limit_bytes=32 * 1024 * 1024),
        cost_estimate=pl.CostEstimate(
            flops=0, bytes_accessed=4 * count * step * width, transcendentals=0
        ),
    )(*arrays)


def pack_small(rate_weight, input_weight, small):
    heads, block, _ = rate_weight.shape
    rows = heads * block
    by_head = jnp.moveaxis(small.reshape(8, heads, block), 1, 0)
    by_head = jnp.pad(by_head, ((0, 0), (0, 8), (0, 0))).reshape(heads * 16, block)

    def kernel(rate, gate_in, values, out):
        for h in range(heads):
            out[0, h * block : (h + 1) * block] = rate[h]
            out[1, h * block : (h + 1) * block] = gate_in[h]
        rest = values[...]
        for t in range(3):
            high = rest.astype(BF16)
            at = rows + t * heads * 16
            out[0, at : at + heads * 16] = high
            out[1, at : at + heads * 16] = high
            rest = rest - high.astype(F32)

    return pl.pallas_call(
        kernel,
        out_shape=jax.ShapeDtypeStruct((2, rows + 48 * heads, block), BF16),
        cost_estimate=pl.CostEstimate(flops=0, bytes_accessed=8 * rows * block, transcendentals=0),
    )(rate_weight, input_weight, by_head)


def unpack_small(halves, place, per, heads):
    _, _, depth, block = halves.shape
    rows = heads * block
    width = per * rows

    def kernel(which, share, gates, vec):
        row = lax.broadcasted_iota(jnp.int32, (block, width), 0)
        column = lax.broadcasted_iota(jnp.int32, (block, width), 1)
        total = jnp.zeros((16, width), F32)
        for p in range(per):
            for h in range(heads):
                head = p * heads + h
                pick = jnp.where(column == row + head * block, 1.0, 0.0).astype(BF16)
                for g in range(2):
                    part = share[g, p, h * block : (h + 1) * block]
                    gates[g, head * block : (head + 1) * block] = jnp.dot(
                        part, pick, preferred_element_type=F32
                    ).astype(BF16)
                for t in range(3):
                    at = rows + (t * heads + h) * 16
                    total = total + jnp.dot(
                        share[0, p, at : at + 16], pick, preferred_element_type=F32
                    )
        vec[...] = total[0:8]

    return pl.pallas_call(
        kernel,
        grid_spec=pltpu.PrefetchScalarGridSpec(
            num_scalar_prefetch=1,
            grid=(1,),
            in_specs=[pl.BlockSpec((2, per, depth, block), lambda i, which: (0, which[0], 0, 0))],
            out_specs=[
                pl.BlockSpec((2, width, width), lambda i, which: (0, 0, 0)),
                pl.BlockSpec((8, width), lambda i, which: (0, 0)),
            ],
        ),
        out_shape=[
            jax.ShapeDtypeStruct((2, width, width), BF16),
            jax.ShapeDtypeStruct((8, width), F32),
        ],
        compiler_params=pltpu.CompilerParams(vmem_limit_bytes=32 * 1024 * 1024),
        cost_estimate=pl.CostEstimate(
            flops=0, bytes_accessed=4 * width * width, transcendentals=0
        ),
    )(place.astype(jnp.int32)[None], halves)


def decay_terms(rate, slope):
    log_decay = rate * slope
    small = 1.0 / 40320.0
    for div in (5040.0, 720.0, 120.0, 24.0, 6.0, 2.0, 1.0):
        small = small * log_decay + 1.0 / div
    less = jnp.where(log_decay < -0.4, jnp.exp(log_decay) - 1.0, log_decay * small)
    decay = 1.0 + less
    square = -less * (1.0 + decay)
    return decay, square


def split_dot(value, weight):
    high = value.astype(BF16)
    rest = (value - high.astype(F32)).astype(BF16)
    return jnp.dot(high, weight, preferred_element_type=F32) + jnp.dot(
        rest, weight, preferred_element_type=F32
    )


def forward_kernel(order, u, halo, same, vec, gates, conv, rate, gate_in, state, prods, ends, rows, keep_a, keep_b):
    nx, step = u.shape[1], u.shape[2]
    length = nx * step
    rows[0:HALO] = halo[0]
    for i in range(nx):
        rows[HALO + i * step : HALO + (i + 1) * step] = u[0, order[i]].astype(F32)
    filtered = vec[4:5] + rows[HALO : HALO + length] * vec[0:1]
    for k in range(1, TAPS):
        filtered = filtered + rows[HALO - k : HALO - k + length] * same[0, :, k : k + 1] * vec[k : k + 1]
    conv[0] = filtered
    r_gate = jax.nn.sigmoid(split_dot(filtered, gates[0]) + vec[5:6])
    i_gate = jax.nn.sigmoid(split_dot(filtered, gates[1]) + vec[6:7])
    rate[0] = r_gate
    gate_in[0] = i_gate
    decay, square = decay_terms(r_gate, vec[7:8])
    a = decay * same[0, :, 1:2]
    b = jnp.sqrt(square) * i_gate * filtered
    width = a.shape[1]
    tiles = length // 8
    a = a.reshape(tiles, 8, width)
    b = b.reshape(tiles, 8, width)
    row = lax.broadcasted_iota(jnp.int32, (tiles, 8, width), 1)
    for d in (1, 2, 4):
        a_back = jnp.where(row >= d, pltpu.roll(a, d, 1), 1.0)
        b_back = jnp.where(row >= d, pltpu.roll(b, d, 1), 0.0)
        b = b + a * b_back
        a = a * a_back
    keep_a[...] = a.reshape(length, width)
    keep_b[...] = b.reshape(length, width)
    carry_s = jnp.zeros((1, width), F32)
    carry_a = jnp.ones((1, width), F32)
    for t in range(tiles):
        at = keep_a[t * 8 : t * 8 + 8]
        bt = keep_b[t * 8 : t * 8 + 8]
        s = bt + at * carry_s
        p = at * carry_a
        at_row = (t * 8) % step
        state[0, order[t * 8 // step], at_row : at_row + 8] = s
        prods[0, order[t * 8 // step], at_row : at_row + 8] = p
        carry_s = s[7:8]
        carry_a = p[7:8]
    ends[0, 0:1] = carry_a
    ends[0, 1:2] = carry_s
    ends[0, 2:8] = jnp.zeros((6, width), F32)


def reverse_kernel(order, d_state, same, vec, rate, grads, prods, ends, keep_g, keep_a):
    nx, step = d_state.shape[1], d_state.shape[2]
    length = nx * step
    width = rate.shape[2]
    decay, _ = decay_terms(rate[0], vec[7:8])
    a = decay * same[0, :, 1:2]
    keep_a[0:length] = a
    keep_a[length : length + 8] = jnp.ones((8, width), F32)
    for i in range(nx):
        keep_g[i * step : (i + 1) * step] = d_state[0, order[i]].astype(F32)
    first = a[0:1]
    tiles = length // 8
    nxt = keep_a[1 : length + 1].reshape(tiles, 8, width)
    g = keep_g[...].reshape(tiles, 8, width)
    row = lax.broadcasted_iota(jnp.int32, (tiles, 8, width), 1)
    p = nxt
    for d in (1, 2, 4):
        g_ahead = jnp.where(row < 8 - d, pltpu.roll(g, 8 - d, 1), 0.0)
        p_ahead = jnp.where(row < 8 - d, pltpu.roll(p, 8 - d, 1), 1.0)
        g = g + p * g_ahead
        p = p * p_ahead
    keep_g[...] = g.reshape(length, width)
    keep_a[0:length] = p.reshape(length, width)
    carry_g = jnp.zeros((1, width), F32)
    carry_p = jnp.ones((1, width), F32)
    for t in reversed(range(tiles)):
        pt = keep_a[t * 8 : t * 8 + 8]
        gt = keep_g[t * 8 : t * 8 + 8] + pt * carry_g
        pt = pt * carry_p
        grads[0, t * 8 : t * 8 + 8] = gt
        prods[0, t * 8 : t * 8 + 8] = pt
        carry_g = gt[0:1]
        carry_p = pt[0:1]
    ends[0, 0:1] = first * carry_p
    ends[0, 1:2] = first * carry_g
    ends[0, 2:8] = jnp.zeros((6, width), F32)


def final_kernel(
    order, u, halo, same, vec, gates, conv, rate, gate_in, state, prods, start, grads, back, carry,
    d_u, head, d_rate, d_input, sums, rows, tail,
):
    nx, step = u.shape[1], u.shape[2]
    length = nx * step
    width = conv.shape[2]
    d_s = grads[0] + back[0] * carry[0, 0:1]
    for i in range(nx):
        rows[HALO + i * step : HALO + (i + 1) * step] = (
            state[0, order[i]] + prods[0, order[i]] * start[0, 0:1]
        )
    rows[HALO - 1 : HALO] = start[0, 0:1]
    s_prev = rows[HALO - 1 : HALO - 1 + length]
    r_gate, i_gate, filtered = rate[0], gate_in[0], conv[0]
    decay, square = decay_terms(r_gate, vec[7:8])
    inverse = lax.rsqrt(jnp.maximum(square, 1e-37))
    scale = square * inverse
    a = decay * same[0, :, 1:2]
    d_scaled = d_s * i_gate * filtered
    d_log = d_s * s_prev * a - d_scaled * (decay * decay) * inverse
    d_i = d_s * scale * filtered * i_gate * (1.0 - i_gate)
    d_r = d_log * vec[7:8] * r_gate * (1.0 - r_gate)
    d_r_low = d_r.astype(BF16)
    d_i_low = d_i.astype(BF16)
    d_rate[0] = d_r_low
    d_input[0] = d_i_low
    back_dims = (((1,), (1,)), ((), ()))
    d_c = (
        d_s * scale * i_gate
        + lax.dot_general(d_r_low, gates[0], back_dims, preferred_element_type=F32)
        + lax.dot_general(d_i_low, gates[1], back_dims, preferred_element_type=F32)
    )
    rows[0:HALO] = halo[0]
    for i in range(nx):
        rows[HALO + i * step : HALO + (i + 1) * step] = u[0, order[i]].astype(F32)

    def column(value):
        return jnp.sum(value, axis=0, keepdims=True)

    parts = [column(d_c * rows[HALO : HALO + length])]
    tail[0:HALO] = jnp.zeros((HALO, width), F32)
    tail[HALO + length : 2 * HALO + length] = jnp.zeros((HALO, width), F32)
    d_rows = d_c * vec[0:1]
    d_head = jnp.zeros((HALO, width), F32)
    for k in range(1, TAPS):
        masked = d_c * same[0, :, k : k + 1]
        parts.append(column(masked * rows[HALO - k : HALO - k + length]))
        tail[HALO : HALO + length] = masked * vec[k : k + 1]
        d_rows = d_rows + tail[HALO + k : HALO + k + length]
        d_head = d_head + tail[k : k + HALO]
    for i in range(nx):
        d_u[0, order[i]] = d_rows[i * step : (i + 1) * step]
    head[0] = d_head
    parts += [column(d_c), column(d_r), column(d_i), column(d_log * r_gate)]

    @pl.when(pl.program_id(0) == 0)
    def _():
        sums[...] = jnp.zeros_like(sums)

    for i, value in enumerate(parts):
        sums[i : i + 1] += value


def chain_spec(*dims):
    return pl.BlockSpec((1, *dims), lambda i: (i,) + (0,) * len(dims))


def whole_spec(*dims):
    return pl.BlockSpec(dims, lambda i: (0,) * len(dims))


def scan_call(kernel, chains, operands, outs, scratch, flops):
    specs = [pl.BlockSpec(memory_space=pltpu.SMEM)]
    for value, chained in operands[1:]:
        specs.append(chain_spec(*value.shape[1:]) if chained else whole_spec(*value.shape))
    shapes, out_specs = [], []
    for shape, dtype, chained in outs:
        shapes.append(jax.ShapeDtypeStruct(shape, dtype))
        out_specs.append(chain_spec(*shape[1:]) if chained else whole_spec(*shape))
    moved = sum(v.size * v.dtype.itemsize for v, _ in operands)
    moved += sum(s.size * s.dtype.itemsize for s in shapes)
    return pl.pallas_call(
        kernel,
        grid=(chains,),
        in_specs=specs,
        out_specs=out_specs,
        out_shape=shapes,
        scratch_shapes=[pltpu.VMEM(s, F32) for s in scratch],
        compiler_params=pltpu.CompilerParams(vmem_limit_bytes=48 * 1024 * 1024),
        cost_estimate=pl.CostEstimate(flops=flops, bytes_accessed=moved, transcendentals=0),
    )(*[v for v, _ in operands])


def norm_back(weighted, rows_in, scale_vec):
    return scale_vec * weighted - rows_in * scale_vec**3 * jnp.mean(
        weighted * rows_in, axis=-1, keepdims=True
    )


def mix(left, right):
    return jnp.dot(left, right, preferred_element_type=F32)


def mix_back(left, right):
    return lax.dot_general(left, right, (((1,), (1,)), ((), ())), preferred_element_type=F32)


def on_device(
    grid,
    inputs,
    seg_ids,
    norm_in,
    proj_y,
    proj_x,
    conv_weight,
    conv_bias,
    rate_weight,
    rate_bias,
    input_weight,
    input_bias,
    decay_param,
    proj_out,
    norm_mlp,
    mlp_gate,
    mlp_up,
    mlp_down,
    cotangent,
):
    nx, ny, nz, nc = (grid.n[p] for p in "xyzc")
    x, y, z, c = (grid.index(p) for p in "xyzc")
    micro, step, depth = inputs.shape
    chains = micro * ny
    length = nx * step
    shard = proj_x.shape[0]

    gain_in = norm_in.astype(F32)[:, None]
    gain_mlp = norm_mlp.astype(F32)[:, None]

    def gained(matrix, gain):
        return (matrix.astype(F32) * gain).astype(BF16)

    width = proj_x.shape[1] // (nx * ny)
    ff_width = mlp_down.shape[1] // (nx * ny)
    plane = nx * ny * shard
    width = proj_x.shape[1] // (nx * ny)
    ff_width = mlp_down.shape[1] // (nx * ny)
    plane = nx * ny * shard
    slope = -8.0 * jax.nn.softplus(-decay_param)
    slope_back = 8.0 * jax.nn.sigmoid(-decay_param)
    small = jnp.concatenate(
        [conv_weight, conv_bias[None], rate_bias[None], input_bias[None], slope[None]], axis=0
    )
    share = small.shape[1]
    heads, block = rate_weight.shape[0], rate_weight.shape[1]
    per = nz // ny
    packed = pack_small(rate_weight, input_weight, small)
    beside = [grid.shift(seg_ids, "y", r) for r in range(1, ny)]
    weights_in = grid.columns_of(
        [gained(proj_x, gain_in), gained(proj_y, gain_in), proj_out]
    ).reshape(plane, 3 * width)
    mix_all = grid.all_rows(weights_in)
    half = lax.dynamic_index_in_dim(after(packed, weights_in), c, 0, keepdims=False)
    others = lax.optimization_barrier([grid.shift(half, "z", r) for r in range(1, nz)])
    own_rows = grid.turn(after(inputs, weights_in, *beside))
    source = own_rows.astype(F32)
    normed, in_hop = grid.spread(own_rows, *others, normed=True)
    by_z = jnp.stack([half, *others])
    by_z = jnp.stack(
        [
            lax.dynamic_index_in_dim(by_z, (z - y * per - i) % nz, 0, keepdims=False)
            for i in range(per)
        ]
    )
    by_z = after(by_z, *in_hop)
    by_x = grid.place([by_z] + [grid.shift(by_z, "x", r) for r in range(1, nx)], "x")
    by_x = jnp.moveaxis(by_x, 0, 1).reshape(per * nx, *half.shape)
    halves = grid.place([by_x] + [grid.shift(by_x, "c", r) for r in range(1, nc)], "c")
    gates, vec = unpack_small(halves, x, per, heads)
    ahead = grid.rows_ahead(own_rows[:, step - HALO :], vec)
    ahead = jnp.stack([ahead] + [grid.shift(ahead, "y", r) for r in range(1, ny)], axis=1)
    ahead = ahead.reshape(chains * HALO, depth)
    segments = jnp.stack([seg_ids, *beside], axis=1)
    padded = jnp.pad(segments, ((0, 0), (0, 0), (HALO, 0)), constant_values=-1)
    near = lax.dynamic_slice_in_dim(padded, z * length, length + HALO, 2)
    here = near[:, :, HALO:]
    same = [jnp.ones_like(here, dtype=F32)]
    for k in range(1, TAPS):
        same.append((near[:, :, HALO - k : HALO - k + length] == here).astype(F32))
    same = jnp.stack(same + [jnp.zeros_like(same[0])] * (8 - TAPS), axis=-1)
    same = same.reshape(chains, length, 8)
    order = ((x - jnp.arange(nx, dtype=jnp.int32)) % nx).astype(jnp.int32)

    pieces = [gained(mlp_gate, gain_mlp), gained(mlp_up, gain_mlp), mlp_down]
    pieces = [after(p, weights_in) for p in pieces]
    weights_ff = grid.columns_of(pieces, *in_hop, same).reshape(plane, -1)
    wide = ff_width - ff_width // 3
    ff_cuts = [
        grid.all_rows(
            jnp.concatenate(
                [weights_ff[:, i * ff_width + lo : i * ff_width + hi] for i in range(3)], axis=1
            )
        )
        for lo, hi in ((0, wide), (wide, ff_width))
    ]

    mix_all = after(mix_all, vec, same)
    mix_x, mix_y, mix_out = (mix_all[:, i * width : (i + 1) * width] for i in range(3))
    drive = mix(normed, mix_x).astype(BF16).reshape(chains, nx, step, width)
    ahead = ahead.astype(F32)
    ahead = ahead * lax.rsqrt(jnp.mean(ahead * ahead, axis=-1, keepdims=True) + NORM_EPS)
    halo = mix(ahead.astype(BF16), mix_x).astype(BF16).reshape(chains, HALO, width).astype(F32)
    own_cot = grid.turn(after(cotangent, drive))
    pre_y = mix(normed, mix_y)
    branch_y, gelu_y_back = jax.vjp(jax.nn.gelu, pre_y)
    shape = (chains, length, width)
    turned = (chains, nx, step, width)
    conv, rate, gate_in, state, prods, ends = scan_call(
        forward_kernel,
        chains,
        [(order, False), (drive, True), (halo, True), (same, True), (vec, False), (gates, False)],
        [(shape, F32, True)] * 3 + [(turned, F32, True)] * 2 + [((chains, 8, width), F32, True)],
        [(length + HALO, width), (length, width), (length, width)],
        flops=8 * chains * length * width * width,
    )

    def carry_from(summary, sign):
        carry = jnp.zeros((chains, 1, width), F32)
        for r in reversed(range(1, nz)):
            got = grid.shift(summary, "z", sign * r, wrap=False)
            carry = got[:, 1:2] + got[:, 0:1] * carry
        return carry

    rows_cot, cot_hop = grid.spread(own_cot, ends)
    start = carry_from(ends[:, 0:2], 1)
    hidden = (state + prods * start[:, None]).astype(BF16)
    hidden_f = hidden.reshape(chains * length, width).astype(F32)
    mixed = after((branch_y * hidden_f).astype(BF16), *cot_hop)
    resid = source + grid.collect(mix_back(mixed, mix_out).astype(BF16), micro)

    scale_mlp = lax.rsqrt(jnp.mean(resid * resid, axis=-1, keepdims=True) + NORM_EPS)
    normed_mlp, _ = grid.spread((resid * scale_mlp).astype(BF16))
    part_mlp, mines, outward, last = 0.0, [], [], ()
    for ff in ff_cuts:
        cut = ff.shape[1] // 3
        ff = after(ff, normed_mlp, *last)
        ff_in, ff_down = ff[:, : 2 * cut], ff[:, 2 * cut :]
        pre_ff = mix(normed_mlp, ff_in).astype(BF16)
        pre_gate, pre_up = pre_ff[:, :cut].astype(F32), pre_ff[:, cut:].astype(F32)
        activated, gelu_gate_back = jax.vjp(jax.nn.gelu, pre_gate)
        product = (activated * pre_up).astype(BF16)
        sum_down = WeightSum(grid, rows_cot, product)
        sum_down.lend()
        grad_prod = mix(rows_cot, after(ff_down, *sum_down.lent))
        grad_gate = gelu_gate_back(grad_prod * pre_up)[0].astype(BF16)
        grad_up = (grad_prod * activated).astype(BF16)
        grad_ff = jnp.concatenate([grad_gate, grad_up], axis=1)
        sum_ff = WeightSum(grid, normed_mlp, grad_ff)
        sum_ff.lend()
        sum_down.right = after(product, *sum_ff.lent)
        sum_down.meet()
        part_mlp = part_mlp + mix_back(after(grad_ff, sum_down.mine), ff_in)
        sum_ff.right = after(grad_ff, part_mlp)
        sum_ff.meet()
        mines += [sum_ff.mine.astype(BF16), sum_down.mine.astype(BF16)]
        outward.append((product, ff_down))
        last = (part_mlp, sum_ff.mine)
    part_mlp = part_mlp.astype(BF16)
    sum_ff.mine = jnp.concatenate(mines, axis=1)
    sum_ff.along_z()
    weighted_mlp = grid.collect(part_mlp, micro, sum_ff.mine)
    grad_resid = own_cot.astype(F32) + norm_back(weighted_mlp, resid, scale_mlp)
    part_out = sum(mix_back(after(left, weighted_mlp), right) for left, right in outward)
    part_out = part_out.astype(BF16)
    grad_branch, _ = grid.spread(grad_resid.astype(BF16), part_out)
    block_out = resid + grid.collect(after(part_out, grad_branch), micro)

    grad_mixed = mix(grad_branch, mix_out)
    grad_pre_y = gelu_y_back(grad_mixed * hidden_f)[0].astype(BF16)
    grad_state = (grad_mixed * branch_y).astype(BF16).reshape(turned)
    d_local, d_prods, d_ends = scan_call(
        reverse_kernel,
        chains,
        [(order, False), (grad_state, True), (same, True), (vec, False), (rate, True)],
        [(shape, F32, True)] * 2 + [((chains, 8, width), F32, True)],
        [(length, width), (length + HALO, width)],
        flops=40 * chains * length * width,
    )
    d_carry = carry_from(d_ends[:, 0:2], -1)
    d_drive, head, *d_pre, sums = scan_call(
        final_kernel,
        chains,
        [
            (order, False),
            (drive, True),
            (halo, True),
            (same, True),
            (vec, False),
            (gates, False),
            (conv, True),
            (rate, True),
            (gate_in, True),
            (state, True),
            (prods, True),
            (start, True),
            (d_local, True),
            (d_prods, True),
            (d_carry, True),
        ],
        [
            (turned, F32, True),
            ((chains, HALO, width), F32, True),
            (shape, BF16, True),
            (shape, BF16, True),
            ((8, width), F32, False),
        ],
        [(length + HALO, width), (length + 2 * HALO, width)],
        flops=8 * chains * length * width * width,
    )
    behind = after(grid.shift(head, "z", -1, wrap=False), block_out)
    chunk = lax.broadcasted_iota(jnp.int32, (1, nx, 1, 1), 1)
    tail = jnp.pad(behind, ((0, 0), (step - HALO, 0), (0, 0)))[:, None]
    d_drive = d_drive + jnp.where(chunk == (x - (nx - 1)) % nx, tail, 0.0)
    grad_drive = d_drive.astype(BF16).reshape(chains * length, width)
    part_in = (mix_back(grad_pre_y, mix_y) + mix_back(grad_drive, mix_x)).astype(BF16)
    both = jnp.concatenate([grad_pre_y, grad_drive], axis=1)
    sum_in = WeightSum(grid, normed, after(both, part_in))
    sum_out = WeightSum(grid, grad_branch, after(mixed, part_in))
    sum_in.lend()
    sum_out.lend()
    sum_in.meet()
    sum_out.meet()
    sum_in.mine = jnp.concatenate([sum_in.mine.astype(BF16), sum_out.mine.astype(BF16)], axis=1)
    conv_low = after(conv, part_in).reshape(chains * length, width).astype(BF16)
    gate_dense = [
        lax.dot_general(
            conv_low,
            d.reshape(chains * length, width),
            (((0,), (0,)), ((), ())),
            preferred_element_type=F32,
        )
        for d in d_pre
    ]
    rest = jnp.zeros((8, block), F32)
    blocks = []
    for h in range(per * heads):
        at = slice(h * block, (h + 1) * block)
        blocks.append(jnp.concatenate([gate_dense[0][at, at], sums[:, at], rest], axis=0))
        blocks.append(jnp.concatenate([gate_dense[1][at, at], rest, rest], axis=0))
    blocks = jnp.stack(blocks).astype(BF16).reshape(per, heads, 2, block + 16, block)
    kept = lax.dynamic_index_in_dim(blocks, c, 2, keepdims=False).astype(F32)
    for r in range(1, nc):
        given = lax.dynamic_index_in_dim(blocks, (c + r) % nc, 2, keepdims=False)
        kept = kept + grid.shift(given, "c", r).astype(F32)
    blocks = kept.astype(BF16)
    weighted_in = grid.collect(part_in, micro, sum_in.mine, blocks)
    weighted_in = after(weighted_in, sum_ff.done)
    sum_in.along_z(sum_ff.done)
    grad_gate_w, grad_up_w, grad_down_w = sum_ff.finish(
        *(
            [(i * wide, wide), (3 * wide + i * (ff_width - wide), ff_width - wide)]
            for i in range(3)
        )
    )
    block_out = grid.turn(block_out.astype(BF16), back=True)
    grad_y_w, grad_x_w, grad_out_w = sum_in.finish(*([(i * width, width)] for i in range(3)))
    scale_in = lax.rsqrt(jnp.mean(source * source, axis=-1, keepdims=True) + NORM_EPS)
    grad_source = grad_resid + norm_back(weighted_in, source, scale_in)
    grad_source = grid.turn(grad_source.astype(BF16), back=True)

    def gain_grad(*pairs):
        return sum(jnp.sum(w.astype(F32) * g, axis=1) for w, g in pairs)

    grad_norm_in = gain_grad((proj_y, grad_y_w), (proj_x, grad_x_w))
    grad_norm_mlp = gain_grad((mlp_gate, grad_gate_w), (mlp_up, grad_up_w))

    blocks = grid.total(blocks, "z", grad_gate_w)
    got = [
        [grid.shift_plane(blocks, ry, rx) if ry or rx else blocks for rx in range(nx)]
        for ry in range(ny)
    ]
    by_y = grid.place([grid.place(row, "x") for row in got], "y")
    mine = lax.dynamic_index_in_dim(
        by_y.reshape(ny * nx * per, *blocks.shape[1:]), z * nx + x, 0, keepdims=False
    )
    mats = grid.gather(mine, "c").astype(F32)
    sums_own = jnp.moveaxis(mats[0, :, block : block + 8], 0, 1).reshape(8, share)
    mats = mats[:, :, :block]
    return (
        block_out,
        grad_source,
        grad_norm_in,
        grad_y_w * gain_in,
        grad_x_w * gain_in,
        sums_own[0:4],
        sums_own[4],
        mats[0],
        sums_own[5],
        mats[1],
        sums_own[6],
        sums_own[7] * slope_back,
        grad_out_w,
        grad_norm_mlp,
        grad_gate_w * gain_mlp,
        grad_up_w * gain_mlp,
        grad_down_w,
    )


def solution(mesh):
    grid = Grid(mesh.shape["seq"], mesh.shape["blk"])
    every = ("seq", "blk")
    placed = (
        P(None, every, None),
        P(None, "seq"),
        P(every),
        P(every, None),
        P(every, None),
        P(None, "blk"),
        P("blk"),
        P("blk", None, None),
        P("blk"),
        P("blk", None, None),
        P("blk"),
        P("blk"),
        P(every, None),
        P(every),
        P(every, None),
        P(every, None),
        P(every, None),
        P(None, every, None),
    )
    return jax.shard_map(
        functools.partial(on_device, grid),
        mesh=mesh,
        in_specs=placed,
        out_specs=(
            P(None, every, None),
            P(None, every, None),
            P(every),
            P(every, None),
            P(every, None),
            P(None, "blk"),
            P("blk"),
            P("blk", None, None),
            P("blk"),
            P("blk", None, None),
            P("blk"),
            P("blk"),
            P(every, None),
            P(every),
            P(every, None),
            P(every, None),
            P(every, None),
        ),
        check_vma=False,
    )
```
